512 devices in a mesh: slab: 128 (over z, y, core), sub: 4 (over x).
Axes of the slice: x: 4, y: 4, z: 16, core: 2. Of those that a mesh axis runs over, the one named last changes fastest.
Arguments:
- features: bfloat16 [4096, 128, 512], P('slab', 'sub'), may hold values from -6 to 6
- cotangent: bfloat16 [4096, 128, 512], P('slab', 'sub'), may hold values from -6 to 6
- weight: bfloat16 [64, 1728], replicated, may hold values from -0.15625 to 0.15625
- occupancy: int32 [512, 16], P('slab', 'sub'), may hold values from 0 to 1, as said below
Outputs:
- out_features: bfloat16 [4096, 128, 512], P('slab', 'sub')
- in_grad: bfloat16 [4096, 128, 512], P('slab', 'sub')
- weight_grad: float32 [64, 1728], replicated
The draws below stay inside these ranges and needn't reach their ends.
Inputs may be any that keep to these rules, and one draw needn't show every extreme that they name: `occupancy`: 1 marks an occupied brick, 0 an empty one. Every aligned block of 4 x 4 brick slots holds at least one occupied brick.
All inputs are finite; a program needn't handle non-finite values.
Results may differ from the reference program's by a relative error of at most 0.001.
Values may be sent and summed in bfloat16 or wider, within the bound.
A program may use at most 128 MiB of HBM per device.

```python
import jax
import jax.numpy as jnp
from jax import lax

C = 64
BRICK = 8
TAPS = 27
BZ = 4
BY = 4
NBZ = 512
NBY = 16
NZV = 4096
NYV = 128
XC = 512
VOXELS = 4194304


def draw_occupancy(key, part):
    key = jax.random.fold_in(key, 11)
    level_key, brick_key, pick_key = jax.random.split(key, 3)
    levels = jax.random.randint(level_key, (NBZ // BZ, NBY // BY), 1, 9)
    levels = jnp.repeat(jnp.repeat(levels, BZ, 0), BY, 1)
    throws = jax.random.randint(brick_key, (NBZ, NBY), 0, 8)
    chosen = jax.random.randint(pick_key, (NBZ // BZ, NBY // BY), 0, BZ * BY)
    chosen = jnp.repeat(jnp.repeat(chosen, BZ, 0), BY, 1)
    row_index = jnp.arange(NBZ, dtype=jnp.int32)[:, None] % BZ
    column_index = jnp.arange(NBY, dtype=jnp.int32)[None, :] % BY
    forced = row_index * BY + column_index == chosen
    return ((throws < levels) | forced).astype(jnp.int32)


def block_scale(stream_key, extent, shards, least, high):
    gain, own = 1.0, jax.random.fold_in(stream_key, 6)
    for position, shards_of in shards:
        heights = jnp.exp(jax.random.uniform(jax.random.fold_in(own, position), (shards_of,), jnp.float32, least / len(shards), high / len(shards)))
        gain = gain * jnp.repeat(heights, extent[position] // shards_of).reshape([-1 if axis == position else 1 for axis in range(len(extent))])
    return gain


def noise(own_key, dims, spread, most, shards=(), kind=jnp.bfloat16):
    drawn = jax.random.normal(own_key, dims, jnp.float32) * spread
    if len(shards) > 0:
        drawn = block_scale(own_key, dims, shards, -0.22, 0.18) * drawn
    return jnp.clip(drawn, min=-most, max=most).astype(kind)


def setup_inputs(seed: int = 0) -> dict:
    splits = jax.random.split(jax.random.key(seed), 5)
    features = noise(splits[0], (NZV, NYV, XC), 1.0, 6.0, ((0, 128), (1, 4)))
    cotangent = noise(splits[1], (NZV, NYV, XC), 1.0, 6.0, ((0, 128), (1, 4)))
    weight = noise(splits[2], (C, TAPS * C), (TAPS * C) ** -0.5, 0.15625)
    occupancy = draw_occupancy(jax.random.fold_in(splits[4], 71), 0)
    return {"features": features, "cotangent": cotangent, "weight": weight, "occupancy": occupancy}


def reference(features, cotangent, weight, occupancy):
    depth_cells, across_cells = features.shape[0], features.shape[1]
    live_plane = jnp.repeat(jnp.repeat(occupancy, BRICK, 0), BRICK, 1).astype(jnp.bfloat16)
    voxel_live = live_plane[:, :, None, None]
    masked_in = features.reshape(depth_cells, across_cells, BRICK, C) * voxel_live
    masked_grad = cotangent.reshape(depth_cells, across_cells, BRICK, C) * voxel_live
    widths = ((1, 1), (1, 1), (1, 1), (0, 0))
    padded_in = jnp.pad(masked_in, widths)
    padded_grad = jnp.pad(masked_grad, widths)
    tap_weights = weight.astype(jnp.float32).reshape(C, TAPS, C)
    highest = lax.Precision.HIGHEST

    def one_layer(totals, layer_index):
        first_row = layer_index * BRICK
        in_slab = lax.dynamic_slice_in_dim(padded_in, first_row, BRICK + 2, 0).astype(jnp.float32)
        grad_slab = lax.dynamic_slice_in_dim(padded_grad, first_row, BRICK + 2, 0).astype(jnp.float32)
        layer_live = lax.dynamic_slice_in_dim(live_plane, first_row, BRICK, 0).astype(jnp.float32)
        layer_mask = jnp.broadcast_to(layer_live[:, :, None], (BRICK, across_cells, BRICK)).reshape(-1, 1)
        center = grad_slab[1:BRICK + 1, 1:across_cells + 1, 1:BRICK + 1].reshape(-1, C)
        output = jnp.zeros((BRICK * across_cells * BRICK, C), jnp.float32)
        input_grad = jnp.zeros((BRICK * across_cells * BRICK, C), jnp.float32)
        tap_terms = []
        for shift_z in range(3):
            for shift_y in range(3):
                for shift_x in range(3):
                    tap_index = 9 * shift_z + 3 * shift_y + shift_x
                    window = in_slab[shift_z:shift_z + BRICK, shift_y:shift_y + across_cells, shift_x:shift_x + BRICK].reshape(-1, C)
                    mirror = grad_slab[2 - shift_z:2 - shift_z + BRICK, 2 - shift_y:2 - shift_y + across_cells, 2 - shift_x:2 - shift_x + BRICK].reshape(-1, C)
                    output = output + jnp.dot(window, tap_weights[:, tap_index, :].T, precision=highest)
                    input_grad = input_grad + jnp.dot(mirror, tap_weights[:, tap_index, :], precision=highest)
                    tap_terms.append(jnp.dot(center.T, window, precision=highest))
        output = (output * layer_mask).astype(jnp.bfloat16)
        input_grad = (input_grad * layer_mask).astype(jnp.bfloat16)
        return totals + jnp.concatenate(tap_terms, axis=1), (output, input_grad)

    totals, (outputs, grad_layers) = lax.scan(one_layer, jnp.zeros((C, TAPS * C), jnp.float32), jnp.arange(depth_cells // BRICK, dtype=jnp.int32))
    out_features = outputs.reshape(depth_cells, across_cells, BRICK * C)
    in_grad = grad_layers.reshape(depth_cells, across_cells, BRICK * C)
    weight_grad = totals * (VOXELS ** -0.5)
    return out_features, in_grad, weight_grad
```

```python
import functools

import jax
import jax.numpy as jnp
from jax import lax
from jax.experimental import pallas as pl
from jax.experimental.pallas import tpu as pltpu
from jax.sharding import PartitionSpec as P

C = 64
BRICK = 8
ROWS = 32
XC = 512
PADX = XC + 2 * C
WINDOW = 384
TAPS = 27
MESH = pl.DeviceIdType.MESH
PLANE = 32
PIECES = 8
CHUNK = 512
WIDE = 4 * CHUNK

FACES_Z = ((1, 0), (-1, 0))
FACES_Y = ((0, 1), (0, -1))
CORNERS = ((1, 1), (1, -1), (-1, 1), (-1, -1))
DIRECTIONS = FACES_Z + FACES_Y + CORNERS


def widen(rows):
    side = jnp.zeros(rows.shape[:-1] + (C,), rows.dtype)
    return jnp.concatenate([side, rows, side], axis=-1)


def build_masks(occ_ref, mask_ref):
    row = lax.broadcasted_iota(jnp.int32, (ROWS, XC), 0) // BRICK
    for brick_z in range(ROWS // BRICK):
        mask = jnp.zeros((ROWS, XC), jnp.float32)
        for brick_y in range(ROWS // BRICK):
            flag = occ_ref[brick_z, brick_y].astype(jnp.float32)
            mask = jnp.where(row == brick_y, flag, mask)
        mask_ref[brick_z] = mask


def build_weights(w_ref, forward_ref, backward_ref):
    for ab in range(9):
        taps = w_ref[:, 192 * ab : 192 * ab + 192]
        for x in range(4):
            parts = [taps]
            if x > 0:
                parts = [jnp.zeros((C, C * x), taps.dtype)] + parts
            if x < 3:
                parts = parts + [jnp.zeros((C, C * (3 - x)), taps.dtype)]
            forward_ref[C * x : C * x + C, WINDOW * ab : WINDOW * ab + WINDOW] = (
                jnp.concatenate(parts, axis=1)
            )
        mirrored = 8 - ab
        for x in range(6):
            low = C * (x - 2)
            first, last = max(0, -low), min(192, 256 - low)
            parts = [taps[:, first:last]]
            if low > 0:
                parts = [jnp.zeros((C, low), taps.dtype)] + parts
            end = low + last
            if end < 256:
                parts = parts + [jnp.zeros((C, 256 - end), taps.dtype)]
            start = WINDOW * mirrored + C * x
            backward_ref[start : start + C, :] = jnp.concatenate(parts, axis=1)


def convolve(shifted_ref, weight_ref, transposed, mask_ref, out_ref, layers=8):
    contract = (((1,), (1 if transposed else 0,)), ((), ()))

    def block(step, _):
        first = step * layers
        mask = mask_ref[first // BRICK, :, :256]
        for quad in range(2):
            window = jnp.concatenate(
                [
                    shifted_ref[
                        b,
                        pl.ds(pl.multiple_of((first + a) * ROWS, ROWS), layers * ROWS),
                        256 * quad : 256 * quad + WINDOW,
                    ]
                    for a in range(3)
                    for b in range(3)
                ],
                axis=1,
            )
            total = lax.dot_general(
                window, weight_ref[...], contract, preferred_element_type=jnp.float32
            )
            total = total.reshape(layers, ROWS, 256) * mask[None]
            out_ref[pl.ds(first, layers), :, 256 * quad : 256 * quad + 256] = total.astype(
                jnp.bfloat16
            )
        return 0

    lax.fori_loop(0, ROWS // layers, block, 0)


def kernel_gradient(turned_ref, shifted_ref, share_ref):
    depth = ROWS + 2
    share_ref[:, TAPS * C :] = jnp.zeros((C, WIDE - TAPS * C), jnp.float32)
    for b in range(3):
        turned = jnp.concatenate(
            [
                turned_ref[:, 128 * (2 - a) : 128 * (2 - a) + 128 * depth]
                for a in range(3)
            ],
            axis=0,
        )
        window = jnp.concatenate(
            [
                shifted_ref[b, ROWS * z : ROWS * z + ROWS, 128 * p : 128 * p + 256]
                for z in range(depth)
                for p in range(4)
            ],
            axis=0,
        )
        product = jnp.dot(turned, window, preferred_element_type=jnp.float32)
        for a in range(3):
            ab = 3 * a + b
            even = product[128 * a : 128 * a + C, :192]
            odd = product[128 * a + C : 128 * a + 2 * C, C : C + 192]
            share_ref[:, 192 * ab : 192 * ab + 192] = even + odd


def mask_and_turn(raw_refs, mask_ref, padded_refs, edge_refs, turned_ref):
    turned_ref[:, :256] = jnp.zeros((128, 256), turned_ref.dtype)
    turned_ref[:, 128 * (ROWS + 2) :] = jnp.zeros((128, 256), turned_ref.dtype)

    def layer(z, _):
        mask = mask_ref[z // BRICK]
        for tensor in range(2):
            slab = raw_refs[tensor][z].astype(jnp.float32) * mask
            padded_refs[tensor][z + 1, 8:40, :] = widen(slab)
            edge_refs[tensor][0, pl.ds(z, 1), :] = slab[:1]
            edge_refs[tensor][1, pl.ds(z, 1), :] = slab[ROWS - 1 :]
            if tensor == 1:
                rows = jnp.concatenate(
                    [slab[:, 128 * p : 128 * p + 128] for p in range(4)], axis=0
                )
                column = pl.ds(pl.multiple_of(128 * (z + 2), 128), 128)
                turned_ref[:, column] = rows.T.astype(jnp.bfloat16)
        return 0

    lax.fori_loop(0, ROWS, layer, 0)


def shift_rows(padded_ref, shifted_ref):
    def layer(z, _):
        rows = pl.ds(pl.multiple_of(z * ROWS, ROWS), ROWS)
        for b in range(3):
            shifted_ref[b, rows, :] = padded_ref[z, 7 + b : 39 + b, :].astype(jnp.bfloat16)
        return 0

    lax.fori_loop(0, ROWS + 2, layer, 0)


def barrier(partners):
    semaphore = pltpu.get_barrier_semaphore()
    total = 0
    for count, partner in partners:
        total += count

        def greet(index, _, partner=partner):
            pl.semaphore_signal(
                semaphore, inc=1, device_id=partner(index), device_id_type=MESH
            )
            return 0

        lax.fori_loop(0, count, greet, 0)
    pl.semaphore_wait(semaphore, total)


def neighbour(direction):
    slabs, subs = lax.axis_size("slab"), lax.axis_size("sub")
    slab = lax.rem(lax.axis_index("slab") + direction[0] + slabs, slabs)
    sub = lax.rem(lax.axis_index("sub") + direction[1] + subs, subs)
    return slab, sub


def exchange(raw, masks, padded_refs, edge_refs, buffers, send_sem, recv_sem):
    face_send, face_recv, edge_send, edge_recv, corner_send, corner_recv = buffers
    slab, sub = lax.axis_index("slab"), lax.axis_index("sub")
    slabs, subs = lax.axis_size("slab"), lax.axis_size("sub")

    for side, (z, row) in enumerate(((ROWS, 0), (1, 1))):
        for tensor in range(2):
            face = padded_refs[tensor][z, 8:40, :]
            face_send[side, tensor] = face.astype(jnp.bfloat16)
            edge = edge_refs[tensor][1 - side]
            edge_send[side, tensor] = edge.astype(jnp.bfloat16)
    for index, (dz, dy) in enumerate(CORNERS):
        z = ROWS - 1 if dz > 0 else 0
        y = 1 if dy > 0 else 0
        corner_send[index] = jnp.concatenate(
            [edge_refs[0][y, z : z + 1, :], edge_refs[1][y, z : z + 1, :]]
            + [jnp.zeros((6, XC), jnp.float32)],
            axis=0,
        )

    copies = []
    for index, direction in enumerate(DIRECTIONS):
        if index < 2:
            source, target = face_send.at[index], face_recv.at[index]
        elif index < 4:
            source, target = edge_send.at[index - 2], edge_recv.at[index - 2]
        else:
            source, target = corner_send.at[index - 4], corner_recv.at[index - 4]
        copy = pltpu.make_async_remote_copy(
            src_ref=source,
            dst_ref=target,
            send_sem=send_sem.at[index],
            recv_sem=recv_sem.at[index],
            device_id=neighbour(direction),
            device_id_type=MESH,
        )
        copy.start()
        copies.append(copy)

    def within(direction):
        dz, dy = direction
        inside = jnp.int32(1)
        if dz:
            inside = inside * jnp.where(slab == (0 if dz > 0 else slabs - 1), 0, 1)
        if dy:
            inside = inside * jnp.where(sub == (0 if dy > 0 else subs - 1), 0, 1)
        return inside.astype(jnp.float32)

    def place():
        for copy in copies:
            copy.wait()
        for index, direction in enumerate(FACES_Z):
            layer = 0 if index == 0 else ROWS + 1
            for tensor in range(2):
                face = face_recv[index, tensor].astype(jnp.float32) * within(direction)
                padded_refs[tensor][layer, 8:40, :] = face
        for index, direction in enumerate(FACES_Y):
            row = 7 if index == 0 else 40
            for tensor in range(2):
                edge_refs[tensor][index] = edge_recv[index, tensor].astype(
                    jnp.float32
                ) * within(direction)
        for index, direction in enumerate(CORNERS):
            layer = 0 if direction[0] > 0 else ROWS + 1
            row = 7 if direction[1] > 0 else 40
            for tensor in range(2):
                corner = corner_recv[index, tensor : tensor + 1, :] * within(direction)
                padded_refs[tensor][layer, row : row + 1, :] = widen(corner)

        def layer_edges(z, _):
            for side, row in enumerate((7, 40)):
                for tensor in range(2):
                    edge = edge_refs[tensor][side, pl.ds(z, 1), :]
                    padded_refs[tensor][z + 1, row : row + 1, :] = widen(edge)
            return 0

        lax.fori_loop(0, ROWS, layer_edges, 0)

    return place


def convolution_kernel(
    features_hbm,
    cotangent_hbm,
    weight_ref,
    occ_ref,
    out_ref,
    grad_ref,
    share_ref,
    features_ref,
    cotangent_ref,
    mask_ref,
    padded_in,
    padded_grad,
    edge_in,
    edge_grad,
    shifted_in,
    shifted_grad,
    turned_ref,
    forward_ref,
    backward_ref,
    face_send,
    face_recv,
    edge_send,
    edge_recv,
    corner_send,
    corner_recv,
    load_sem,
    send_sem,
    recv_sem,
):
    loads = [
        pltpu.make_async_copy(features_hbm, features_ref, load_sem.at[0]),
        pltpu.make_async_copy(cotangent_hbm, cotangent_ref, load_sem.at[1]),
    ]
    for load in loads:
        load.start()
    semaphore = pltpu.get_barrier_semaphore()
    for direction in DIRECTIONS:
        pl.semaphore_signal(
            semaphore, inc=1, device_id=neighbour(direction), device_id_type=MESH
        )
    build_masks(occ_ref, mask_ref)
    for load in loads:
        load.wait()
    padded_refs, edge_refs = (padded_in, padded_grad), (edge_in, edge_grad)
    mask_and_turn(
        (features_ref, cotangent_ref), mask_ref, padded_refs, edge_refs, turned_ref
    )
    pl.semaphore_wait(semaphore, len(DIRECTIONS))
    buffers = (face_send, face_recv, edge_send, edge_recv, corner_send, corner_recv)
    place = exchange(
        (features_ref, cotangent_ref), mask_ref, padded_refs, edge_refs, buffers, send_sem, recv_sem
    )
    build_weights(weight_ref, forward_ref, backward_ref)
    place()
    shift_rows(padded_in, shifted_in)
    kernel_gradient(turned_ref, shifted_in, share_ref)
    shift_rows(padded_grad, shifted_grad)
    convolve(shifted_in, forward_ref, True, mask_ref, out_ref)
    convolve(shifted_grad, backward_ref, False, mask_ref, grad_ref)


def convolution_scratch():
    bf16, f32 = jnp.bfloat16, jnp.float32
    return [
        pltpu.VMEM((ROWS, ROWS, XC), bf16),
        pltpu.VMEM((ROWS, ROWS, XC), bf16),
        pltpu.VMEM((ROWS // BRICK, ROWS, XC), f32),
        pltpu.VMEM((ROWS + 2, 48, PADX), f32),
        pltpu.VMEM((ROWS + 2, 48, PADX), f32),
        pltpu.VMEM((2, ROWS, XC), f32),
        pltpu.VMEM((2, ROWS, XC), f32),
        pltpu.VMEM((3, (ROWS + 2) * ROWS, PADX), bf16),
        pltpu.VMEM((3, (ROWS + 2) * ROWS, PADX), bf16),
        pltpu.VMEM((128, 128 * (ROWS + 4)), bf16),
        pltpu.VMEM((256, 9 * WINDOW), bf16),
        pltpu.VMEM((9 * WINDOW, 256), bf16),
        pltpu.VMEM((2, 2, ROWS, PADX), bf16),
        pltpu.VMEM((2, 2, ROWS, PADX), bf16),
        pltpu.VMEM((2, 2, ROWS, XC), bf16),
        pltpu.VMEM((2, 2, ROWS, XC), bf16),
        pltpu.VMEM((4, 8, XC), f32),
        pltpu.VMEM((4, 8, XC), f32),
        pltpu.SemaphoreType.DMA((2,)),
        pltpu.SemaphoreType.DMA((8,)),
        pltpu.SemaphoreType.DMA((8,)),
    ]


def plane_partner(index):
    slab, sub = lax.axis_index("slab"), lax.axis_index("sub")
    place = lax.rem(lax.rem(slab, 8) * 4 + sub + index + 1, PLANE)
    return (slab // 8 * 8 + place // 4, lax.rem(place, 4)), place


def column_partner(index):
    slab, sub = lax.axis_index("slab"), lax.axis_index("sub")
    z = lax.rem(slab // 8 + index + 1, lax.axis_size("slab") // 8)
    return (z * 8 + lax.rem(slab, 8), sub), z


def half_partner(index):
    slab, sub = lax.axis_index("slab"), lax.axis_index("sub")
    z = slab // 8
    z = z // PIECES * PIECES + lax.rem(z + index + 1, PIECES)
    return (z * 8 + lax.rem(slab, 8), sub), z


def chunk(ref, place):
    row = pl.multiple_of(place // 4 * 8, 8)
    lane = pl.multiple_of(lax.rem(place, 4) * CHUNK, CHUNK)
    return ref.at[pl.ds(row, 8), pl.ds(lane, CHUNK)]


def spread(count, copy):
    def start(index, _):
        copy(index).start()
        return 0

    lax.fori_loop(0, count, start, 0)


def settle(count, copy):
    def wait(index, _):
        copy(index).wait()
        return 0

    lax.fori_loop(0, count, wait, 0)


def sum_kernel(
    share_ref,
    result_ref,
    plane_recv,
    rows_ref,
    column_recv,
    done_ref,
    full_ref,
    plane_send_sem,
    plane_recv_sem,
    column_send_sem,
    column_recv_sem,
    half_send_sem,
    half_recv_sem,
    gather_send_sem,
    gather_recv_sem,
):
    deep = lax.axis_size("slab") // 8
    slab, sub = lax.axis_index("slab"), lax.axis_index("sub")
    z, place = slab // 8, lax.rem(slab, 8) * 4 + sub
    barrier(
        [
            (PLANE - 1, lambda index: plane_partner(index)[0]),
            (deep - 1, lambda index: column_partner(index)[0]),
        ]
    )

    def to_plane(index):
        device, other = plane_partner(index)
        return pltpu.make_async_remote_copy(
            src_ref=chunk(share_ref, other),
            dst_ref=plane_recv.at[index],
            send_sem=plane_send_sem.at[index],
            recv_sem=plane_recv_sem.at[index],
            device_id=device,
            device_id_type=MESH,
        )

    def to_column(index):
        device, other = column_partner(index)
        return pltpu.make_async_remote_copy(
            src_ref=rows_ref.at[lax.rem(other, PIECES)],
            dst_ref=column_recv.at[index],
            send_sem=column_send_sem.at[index],
            recv_sem=column_recv_sem.at[index],
            device_id=device,
            device_id_type=MESH,
        )

    own = lax.rem(z, PIECES)

    def to_half(index):
        device, _ = half_partner(index)
        return pltpu.make_async_remote_copy(
            src_ref=done_ref.at[own],
            dst_ref=done_ref.at[own],
            send_sem=half_send_sem.at[index],
            recv_sem=half_recv_sem.at[index],
            device_id=device,
            device_id_type=MESH,
        )

    def to_all(index):
        device, _ = plane_partner(index)
        return pltpu.make_async_remote_copy(
            src_ref=chunk(full_ref, place),
            dst_ref=chunk(full_ref, place),
            send_sem=gather_send_sem.at[index],
            recv_sem=gather_recv_sem.at[index],
            device_id=device,
            device_id_type=MESH,
        )

    spread(PLANE - 1, to_plane)
    settle(PLANE - 1, to_plane)
    total = chunk(share_ref, place)[...]
    for index in range(PLANE - 1):
        total = total + plane_recv[index]
    for row in range(PIECES):
        rows_ref[row] = total[row : row + 1]
    spread(deep - 1, to_column)
    settle(deep - 1, to_column)
    piece = rows_ref[own]
    for index in range(deep - 1):
        piece = piece + column_recv[index]
    done_ref[own] = piece
    spread(PIECES - 1, to_half)
    settle(PIECES - 1, to_half)
    mine = chunk(full_ref, place)
    mine[...] = jnp.concatenate([done_ref[row] for row in range(PIECES)], axis=0)
    spread(PLANE - 1, to_all)
    settle(PLANE - 1, to_all)
    cells = lax.axis_size("slab") * lax.axis_size("sub") * ROWS * ROWS * BRICK
    result_ref[...] = full_ref[:, : TAPS * C] * cells ** (-0.5)


def sum_scratch(deep):
    f32, dma = jnp.float32, pltpu.SemaphoreType.DMA
    return [
        pltpu.VMEM((PLANE - 1, 8, CHUNK), f32),
        pltpu.VMEM((PIECES, 1, CHUNK), f32),
        pltpu.VMEM((deep - 1, 1, CHUNK), f32),
        pltpu.VMEM((PIECES, 1, CHUNK), f32),
        pltpu.VMEM((C, WIDE), f32),
        dma((PLANE - 1,)),
        dma((PLANE - 1,)),
        dma((deep - 1,)),
        dma((deep - 1,)),
        dma((PIECES - 1,)),
        dma((PIECES - 1,)),
        dma((PLANE - 1,)),
        dma((PLANE - 1,)),
    ]


def convolutions(features, cotangent, weight, occupancy):
    vmem, hbm = pl.BlockSpec(memory_space=pltpu.VMEM), pl.BlockSpec(memory_space=pl.ANY)
    return pl.pallas_call(
        convolution_kernel,
        out_shape=[
            jax.ShapeDtypeStruct(features.shape, jnp.bfloat16),
            jax.ShapeDtypeStruct(features.shape, jnp.bfloat16),
            jax.ShapeDtypeStruct((C, WIDE), jnp.float32),
        ],
        in_specs=[hbm, hbm, vmem, pl.BlockSpec(memory_space=pltpu.SMEM)],
        out_specs=[vmem, vmem, vmem],
        scratch_shapes=convolution_scratch(),
        compiler_params=pltpu.CompilerParams(
            collective_id=0, has_side_effects=True, vmem_limit_bytes=56 * 2**20
        ),
        cost_estimate=pl.CostEstimate(
            flops=11 * 10**9, bytes_accessed=5 * 2**20, transcendentals=0
        ),
        name="convolutions",
    )(features, cotangent, weight, occupancy)


def sum_shares(share, deep):
    vmem = pl.BlockSpec(memory_space=pltpu.VMEM)
    return pl.pallas_call(
        sum_kernel,
        out_shape=jax.ShapeDtypeStruct((C, TAPS * C), jnp.float32),
        in_specs=[vmem],
        out_specs=vmem,
        scratch_shapes=sum_scratch(deep),
        compiler_params=pltpu.CompilerParams(
            collective_id=1, has_side_effects=True, vmem_limit_bytes=16 * 2**20
        ),
        cost_estimate=pl.CostEstimate(
            flops=10**7, bytes_accessed=2 * 2**20, transcendentals=0
        ),
        name="sum_shares",
    )(share)


def per_device(features, cotangent, weight, occupancy):
    out, grad, share = convolutions(features, cotangent, weight, occupancy)
    total = sum_shares(share, lax.axis_size("slab") // 8)
    return out, grad, total


def solution(mesh):
    placed = (P("slab", "sub", None), P("slab", "sub", None), P(), P("slab", "sub"))
    return jax.shard_map(
        per_device,
        mesh=mesh,
        in_specs=placed,
        out_specs=(P("slab", "sub", None), P("slab", "sub", None), P()),
        check_vma=False,
    )
```

```python
import jax
import jax.numpy as jnp
from jax import lax
from jax.experimental import pallas as pl
from jax.experimental.pallas import tpu as pltpu
from jax.sharding import PartitionSpec as P

C = 64
BRICK = 8
ROWS = 32
XC = 512
PADX = XC + 2 * C
WINDOW = 384
TAPS = 27
MESH = pl.DeviceIdType.MESH
DEEP = 16
PLANE = 16
PIECES = 4
CHUNK = 512
WIDE = 4 * CHUNK
HALF = C // 2

FACES_Z = ((1, 0), (-1, 0))
FACES_Y = ((0, 1), (0, -1))
CORNERS = ((1, 1), (1, -1), (-1, 1), (-1, -1))
DIRECTIONS = FACES_Z + FACES_Y + CORNERS


def widen(rows):
    side = jnp.zeros(rows.shape[:-1] + (C,), rows.dtype)
    return jnp.concatenate([side, rows, side], axis=-1)


def pairs(rows):
    return jnp.concatenate([rows[:, 128 * p : 128 * p + 128] for p in range(4)], axis=0)


def pair_windows(rows):
    return jnp.concatenate([rows[:, 128 * p : 128 * p + 256] for p in range(4)], axis=0)


def build_masks(occ_ref, mask_ref, narrow_ref):
    row = lax.broadcasted_iota(jnp.int32, (ROWS, XC), 0) // BRICK
    for brick_z in range(ROWS // BRICK):
        mask = jnp.zeros((ROWS, XC), jnp.float32)
        for brick_y in range(ROWS // BRICK):
            flag = occ_ref[brick_z, brick_y].astype(jnp.float32)
            mask = jnp.where(row == brick_y, flag, mask)
        mask_ref[brick_z] = mask
        narrow_ref[brick_z] = mask.astype(jnp.bfloat16)


def build_weights(w_ref, forward_ref, backward_ref):
    for ab in range(9):
        taps = w_ref[:, 192 * ab : 192 * ab + 192]
        for x in range(4):
            parts = [taps]
            if x > 0:
                parts = [jnp.zeros((C, C * x), taps.dtype)] + parts
            if x < 3:
                parts = parts + [jnp.zeros((C, C * (3 - x)), taps.dtype)]
            forward_ref[C * x : C * x + C, WINDOW * ab : WINDOW * ab + WINDOW] = (
                jnp.concatenate(parts, axis=1)
            )
        mirrored = 8 - ab
        for x in range(6):
            low = C * (x - 2)
            first, last = max(0, -low), min(192, 256 - low)
            parts = [taps[:, first:last]]
            if low > 0:
                parts = [jnp.zeros((C, low), taps.dtype)] + parts
            end = low + last
            if end < 256:
                parts = parts + [jnp.zeros((C, 256 - end), taps.dtype)]
            start = WINDOW * mirrored + C * x
            backward_ref[start : start + C, :] = jnp.concatenate(parts, axis=1)


def clear_sides(stage_ref, turned_ref, share_ref):
    for side in range(2):
        stage_ref[side, 0:8, :] = jnp.zeros((8, PADX), jnp.float32)
        stage_ref[side, 40:48, :] = jnp.zeros((8, PADX), jnp.float32)
    for b in range(3):
        turned_ref[b, :, :128] = jnp.zeros((128, 128), turned_ref.dtype)
        turned_ref[b, :, 128 * (ROWS + 1) :] = jnp.zeros((128, 128), turned_ref.dtype)
    share_ref[:, TAPS * C :] = jnp.zeros((C, WIDE - TAPS * C), jnp.float32)


def cut_faces(raw_refs, mask_ref, edge_refs, buffers):
    face_send, _, edge_send, _, corner_send, _ = buffers

    def layer(z, _):
        mask = mask_ref[z // BRICK]
        for tensor in range(2):
            for side, tile in enumerate((0, ROWS - 16)):
                rows = raw_refs[tensor][z, tile : tile + 16, :].astype(jnp.float32)
                row = 0 if side == 0 else 15
                edge_refs[tensor][side, pl.ds(z, 1), :] = (
                    rows[row : row + 1] * mask[tile + row : tile + row + 1]
                )
        return 0

    lax.fori_loop(0, ROWS, layer, 0, unroll=4)
    for side, z in enumerate((ROWS - 1, 0)):
        for tensor in range(2):
            face = raw_refs[tensor][z].astype(jnp.float32) * mask_ref[z // BRICK]
            face_send[side, tensor] = face.astype(jnp.bfloat16)
            edge_send[side, tensor] = edge_refs[tensor][1 - side].astype(jnp.bfloat16)
    for index, (dz, dy) in enumerate(CORNERS):
        z = ROWS - 1 if dz > 0 else 0
        y = 1 if dy > 0 else 0
        corner_send[index] = jnp.concatenate(
            [edge_refs[0][y, z : z + 1, :], edge_refs[1][y, z : z + 1, :]]
            + [jnp.zeros((6, XC), jnp.float32)],
            axis=0,
        )


def prepare(raw_ref, narrow_ref, shifted_ref, unroll=8):
    def layer(z, _):
        rows = pl.ds(pl.multiple_of((z + 1) * ROWS, ROWS), ROWS)
        shifted_ref[1, rows, :] = widen(raw_ref[z] * narrow_ref[z // BRICK])
        return 0

    lax.fori_loop(0, ROWS, layer, 0, unroll=unroll)


def prepare_both(features_ref, cotangent_ref, narrow_ref, shifted_ref, turned_ref):
    edge = jnp.zeros((128, 1), jnp.bfloat16)
    row = lax.broadcasted_iota(jnp.int32, (128, 128), 1) % ROWS
    not_last = (row != ROWS - 1).astype(jnp.float32).astype(jnp.bfloat16)
    not_first = (row != 0).astype(jnp.float32).astype(jnp.bfloat16)

    def layer(z, _):
        mask = narrow_ref[z // BRICK]
        rows = pl.ds(pl.multiple_of((z + 1) * ROWS, ROWS), ROWS)
        shifted_ref[1, rows, :] = widen(features_ref[z] * mask)
        column = pl.ds(pl.multiple_of(128 * (z + 1), 128), 128)
        turned = pairs(cotangent_ref[z] * mask).T
        turned_ref[0, :, column] = not_last * jnp.concatenate([turned[:, 1:], edge], axis=1)
        turned_ref[1, :, column] = turned
        turned_ref[2, :, column] = not_first * jnp.concatenate([edge, turned[:, :127]], axis=1)
        return 0

    lax.fori_loop(0, ROWS, layer, 0, unroll=8)


def pad_rows(shifted_ref, padded_ref):
    def layer(z, _):
        rows = pl.ds(pl.multiple_of((z + 1) * ROWS, ROWS), ROWS)
        padded_ref[z + 1, 8:40, :] = shifted_ref[1, rows, :].astype(jnp.float32)
        return 0

    lax.fori_loop(0, ROWS, layer, 0, unroll=4)


def shift_layer(padded_ref, shifted_ref, z, shifts):
    rows = pl.ds(pl.multiple_of(z * ROWS, ROWS), ROWS)
    for b in shifts:
        shifted_ref[b, rows, :] = padded_ref[z, 7 + b : 39 + b, :].astype(jnp.bfloat16)


def shift_rows(padded_ref, shifted_ref):
    def layer(z, _):
        shift_layer(padded_ref, shifted_ref, z, (0, 2))
        return 0

    lax.fori_loop(1, ROWS + 1, layer, 0, unroll=8)


def inner_gradient(turned_ref, shifted_ref, product_ref):
    window = jnp.concatenate(
        [
            shifted_ref[1, ROWS * z : ROWS * z + ROWS, 128 * p : 128 * p + 256]
            for z in range(1, ROWS + 1)
            for p in range(4)
        ],
        axis=0,
    )
    for b in range(3):
        turned = jnp.concatenate(
            [turned_ref[b, :, 128 * (2 - a) : 128 * (2 - a + ROWS)] for a in range(3)],
            axis=0,
        )
        product_ref[b] = jnp.dot(turned, window, preferred_element_type=jnp.float32)


def outer_gradient(turned_ref, shifted_ref, edge_turned_ref, stage_ref, product_ref, share_ref):
    def along_z(z, layer):
        first = ROWS * layer
        window = jnp.concatenate(
            [pair_windows(shifted_ref[b, first : first + ROWS, :]) for b in range(3)],
            axis=1,
        )
        column = turned_ref[1, :, 128 * (z + 1) : 128 * (z + 2)]
        return jnp.dot(column, window, preferred_element_type=jnp.float32)

    def along_y(side):
        window = jnp.concatenate(
            [
                pair_windows(stage_ref[side, 7 + a : 39 + a, :].astype(jnp.bfloat16))
                for a in range(3)
            ],
            axis=1,
        )
        return jnp.dot(edge_turned_ref[side], window, preferred_element_type=jnp.float32)

    low_z, high_z = along_z(0, 0), along_z(ROWS - 1, ROWS + 1)
    edges = {0: along_y(0), 2: along_y(1)}
    for b in range(3):
        for a in range(3):
            term = product_ref[b, 128 * a : 128 * a + 128, :]
            if a == 0:
                term = term + low_z[:, 256 * b : 256 * b + 256]
            if a == 2:
                term = term + high_z[:, 256 * b : 256 * b + 256]
            if b != 1:
                term = term + edges[b][:, 256 * a : 256 * a + 256]
            ab = 3 * a + b
            share_ref[:, 192 * ab : 192 * ab + 192] = (
                term[:C, :192] + term[C:, C : C + 192]
            )


def convolve(shifted_ref, weight_ref, transposed, mask_ref, out_ref, start, stop, layers=BRICK):
    contract = (((1,), (1 if transposed else 0,)), ((), ()))

    def block(step, _):
        first = step * layers
        mask = mask_ref[first // BRICK, :, :256]
        for quad in range(2):
            window = jnp.concatenate(
                [
                    shifted_ref[
                        b,
                        pl.ds(pl.multiple_of((first + a) * ROWS, ROWS), layers * ROWS),
                        256 * quad : 256 * quad + WINDOW,
                    ]
                    for a in range(3)
                    for b in range(3)
                ],
                axis=1,
            )
            total = lax.dot_general(
                window, weight_ref[...], contract, preferred_element_type=jnp.float32
            )
            total = total.reshape(layers, ROWS, 256) * mask[None]
            out_ref[pl.ds(first, layers), :, 256 * quad : 256 * quad + 256] = total.astype(
                jnp.bfloat16
            )
        return 0

    lax.fori_loop(start, stop, block, 0)


def neighbour(direction):
    slabs, subs = lax.axis_size("slab"), lax.axis_size("sub")
    slab = lax.rem(lax.axis_index("slab") + direction[0] + slabs, slabs)
    sub = lax.rem(lax.axis_index("sub") + direction[1] + subs, subs)
    return slab, sub


def within(direction):
    dz, dy = direction
    inside = jnp.int32(1)
    if dz:
        edge = 0 if dz > 0 else lax.axis_size("slab") - 1
        inside = inside * jnp.where(lax.axis_index("slab") == edge, 0, 1)
    if dy:
        edge = 0 if dy > 0 else lax.axis_size("sub") - 1
        inside = inside * jnp.where(lax.axis_index("sub") == edge, 0, 1)
    return inside.astype(jnp.float32)


def halo_copies(buffers, send_sem, recv_sem):
    face_send, face_recv, edge_send, edge_recv, corner_send, corner_recv = buffers
    copies = []
    for index, direction in enumerate(DIRECTIONS):
        if index < 2:
            source, target = face_send.at[index], face_recv.at[index]
        elif index < 4:
            source, target = edge_send.at[index - 2], edge_recv.at[index - 2]
        else:
            source, target = corner_send.at[index - 4], corner_recv.at[index - 4]
        copies.append(
            pltpu.make_async_remote_copy(
                src_ref=source,
                dst_ref=target,
                send_sem=send_sem.at[index],
                recv_sem=recv_sem.at[index],
                device_id=neighbour(direction),
                device_id_type=MESH,
            )
        )
    return copies


def place_layers(tensor, buffers, padded_ref):
    _, face_recv, _, _, _, corner_recv = buffers
    for index, direction in enumerate(FACES_Z):
        layer = 0 if index == 0 else ROWS + 1
        face = face_recv[index, tensor].astype(jnp.float32) * within(direction)
        padded_ref[layer, 8:40, :] = widen(face)
    for index, direction in enumerate(CORNERS):
        layer = 0 if direction[0] > 0 else ROWS + 1
        row = 7 if direction[1] > 0 else 40
        corner = corner_recv[index, tensor : tensor + 1, :] * within(direction)
        padded_ref[layer, row : row + 1, :] = widen(corner)


def stage_edges(tensor, buffers, stage_ref):
    _, _, _, edge_recv, _, _ = buffers
    for index, direction in enumerate(FACES_Y):
        edge = edge_recv[index, tensor].astype(jnp.float32) * within(direction)
        stage_ref[index, 8:40, :] = widen(edge)


def place_rows(stage_ref, padded_ref):
    def layer(z, _):
        for side, row in enumerate((7, 40)):
            padded_ref[z + 1, row : row + 1, :] = stage_ref[side, pl.ds(8 + z, 1), :]
        return 0

    lax.fori_loop(0, ROWS, layer, 0)


def spread(count, copy):
    def start(index, _):
        copy(index).start()
        return 0

    lax.fori_loop(0, count, start, 0)


def settle(count, copy):
    def wait(index, _):
        copy(index).wait()
        return 0

    lax.fori_loop(0, count, wait, 0)


def sibling():
    slab = lax.axis_index("slab")
    return slab + 1 - 2 * lax.rem(slab, 2), lax.axis_index("sub")


def plane_place():
    return lax.rem(lax.axis_index("slab") // 2, 4) * 4 + lax.axis_index("sub")


def plane_partner(index):
    slab = lax.axis_index("slab")
    place = lax.rem(plane_place() + index + 1, PLANE)
    return (slab // 8 * 8 + place // 4 * 2 + lax.rem(slab, 2), lax.rem(place, 4)), place


def column_partner(step):
    slab = lax.axis_index("slab")
    z = lax.rem(slab // 8 + step + DEEP, DEEP)
    return (z * 8 + lax.rem(slab, 8), lax.axis_index("sub")), z


def chunk(ref, place):
    row = pl.multiple_of(place // 4 * 8, 8)
    lane = pl.multiple_of(lax.rem(place, 4) * CHUNK, CHUNK)
    return ref.at[pl.ds(row, 8), pl.ds(lane, CHUNK)]


def half(ref, core):
    return ref.at[pl.ds(pl.multiple_of(core * HALF, HALF), HALF)]


def greet():
    semaphore = pltpu.get_barrier_semaphore()

    def signal(device):
        pl.semaphore_signal(semaphore, inc=1, device_id=device, device_id_type=MESH)

    def plane(index, _):
        signal(plane_partner(index)[0])
        return 0

    def column(index, _):
        signal(column_partner(index + 1)[0])
        return 0

    for direction in DIRECTIONS:
        signal(neighbour(direction))
    signal(sibling())
    lax.fori_loop(0, PLANE - 1, plane, 0)
    lax.fori_loop(0, DEEP - 1, column, 0)
    return lambda: pl.semaphore_wait(
        semaphore, len(DIRECTIONS) + 1 + (PLANE - 1) + (DEEP - 1)
    )


def kernel(
    features_hbm,
    cotangent_hbm,
    weight_hbm,
    occ_hbm,
    out_ref,
    grad_ref,
    result_ref,
    features_ref,
    cotangent_ref,
    weight_ref,
    occ_ref,
    mask_ref,
    narrow_ref,
    padded_in,
    padded_grad,
    edge_in,
    edge_grad,
    stage_ref,
    shifted_in,
    shifted_grad,
    turned_ref,
    edge_turned_ref,
    forward_ref,
    backward_ref,
    product_ref,
    share_ref,
    face_send,
    face_recv,
    edge_send,
    edge_recv,
    corner_send,
    corner_recv,
    core_recv,
    half_ref,
    plane_recv,
    pieces_ref,
    column_recv,
    done_ref,
    full_ref,
    load_sem,
    halo_send_sem,
    halo_recv_sem,
    core_sem,
    plane_send_sem,
    plane_recv_sem,
    column_send_sem,
    column_recv_sem,
    near_send_sem,
    near_recv_sem,
    gather_send_sem,
    gather_recv_sem,
):
    loads = [
        pltpu.make_async_copy(features_hbm, features_ref, load_sem.at[0]),
        pltpu.make_async_copy(cotangent_hbm, cotangent_ref, load_sem.at[1]),
        pltpu.make_async_copy(weight_hbm, weight_ref, load_sem.at[2]),
    ]
    flags = pltpu.make_async_copy(occ_hbm, occ_ref, load_sem.at[3])
    slab = lax.axis_index("slab")
    z, core, place = slab // 8, lax.rem(slab, 2), plane_place()
    own = lax.rem(z, PIECES)
    buffers = (face_send, face_recv, edge_send, edge_recv, corner_send, corner_recv)
    halos = halo_copies(buffers, halo_send_sem, halo_recv_sem)
    to_sibling = pltpu.make_async_remote_copy(
        src_ref=half(share_ref, 1 - core),
        dst_ref=core_recv,
        send_sem=core_sem.at[0],
        recv_sem=core_sem.at[1],
        device_id=sibling(),
        device_id_type=MESH,
    )

    def to_plane(index):
        device, other = plane_partner(index)
        return pltpu.make_async_remote_copy(
            src_ref=chunk(half_ref, other),
            dst_ref=plane_recv.at[index],
            send_sem=plane_send_sem.at[index],
            recv_sem=plane_recv_sem.at[index],
            device_id=device,
            device_id_type=MESH,
        )

    def to_column(index):
        device, other = column_partner(index + 1)
        return pltpu.make_async_remote_copy(
            src_ref=pieces_ref.at[lax.rem(other, PIECES)],
            dst_ref=column_recv.at[z],
            send_sem=column_send_sem.at[index],
            recv_sem=column_recv_sem.at[index],
            device_id=device,
            device_id_type=MESH,
        )

    def to_near(index):
        device, _ = column_partner((-1, 1, -2)[index])
        return pltpu.make_async_remote_copy(
            src_ref=done_ref.at[own],
            dst_ref=done_ref.at[own],
            send_sem=near_send_sem.at[index],
            recv_sem=near_recv_sem.at[index],
            device_id=device,
            device_id_type=MESH,
        )

    def to_all(index):
        device, _ = plane_partner(index)
        mine = chunk(half(full_ref, core), place)
        return pltpu.make_async_remote_copy(
            src_ref=mine,
            dst_ref=mine,
            send_sem=gather_send_sem.at[index],
            recv_sem=gather_recv_sem.at[index],
            device_id=device,
            device_id_type=MESH,
        )

    back_to_sibling = pltpu.make_async_remote_copy(
        src_ref=half(full_ref, core),
        dst_ref=half(full_ref, core),
        send_sem=core_sem.at[2],
        recv_sem=core_sem.at[3],
        device_id=sibling(),
        device_id_type=MESH,
    )

    flags.start()
    for load in loads:
        load.start()
    everyone_here = greet()
    clear_sides(stage_ref, turned_ref, share_ref)
    flags.wait()
    build_masks(occ_ref, mask_ref, narrow_ref)
    for load in loads:
        load.wait()
    cut_faces((features_ref, cotangent_ref), mask_ref, (edge_in, edge_grad), buffers)
    everyone_here()
    for copy in halos:
        copy.start()

    prepare_both(features_ref, cotangent_ref, narrow_ref, shifted_in, turned_ref)
    for side in range(2):
        edge_turned_ref[side] = pairs(edge_grad[side]).T.astype(jnp.bfloat16)
    inner_gradient(turned_ref, shifted_in, product_ref)

    for copy in halos:
        copy.wait()
    place_layers(0, buffers, padded_in)
    for layer in (0, ROWS + 1):
        shift_layer(padded_in, shifted_in, layer, (0, 1, 2))
    stage_edges(0, buffers, stage_ref)
    outer_gradient(
        turned_ref, shifted_in, edge_turned_ref, stage_ref, product_ref, share_ref
    )
    to_sibling.start()

    build_weights(weight_ref, forward_ref, backward_ref)
    pad_rows(shifted_in, padded_in)
    to_sibling.wait()
    half_ref[...] = half(share_ref, core)[...] + core_recv[...]
    spread(PLANE - 1, to_plane)

    place_rows(stage_ref, padded_in)
    shift_rows(padded_in, shifted_in)
    convolve(shifted_in, forward_ref, True, mask_ref, out_ref, 0, 3)
    settle(PLANE - 1, to_plane)
    total = chunk(half_ref, place)[...]
    for index in range(PLANE - 1):
        total = total + plane_recv[index]
    for piece in range(PIECES):
        pieces_ref[piece] = total[:, 128 * piece : 128 * piece + 128]
    spread(DEEP - 1, to_column)

    convolve(shifted_in, forward_ref, True, mask_ref, out_ref, 3, 4)
    prepare(cotangent_ref, narrow_ref, shifted_grad)
    pad_rows(shifted_grad, padded_grad)
    place_layers(1, buffers, padded_grad)
    stage_edges(1, buffers, stage_ref)
    place_rows(stage_ref, padded_grad)
    shift_rows(padded_grad, shifted_grad)
    for layer in (0, ROWS + 1):
        shift_layer(padded_grad, shifted_grad, layer, (0, 1, 2))
    convolve(shifted_grad, backward_ref, False, mask_ref, grad_ref, 0, 2)
    settle(DEEP - 1, to_column)
    column_recv[z] = pieces_ref[own]
    piece = column_recv[0]
    for index in range(1, DEEP):
        piece = piece + column_recv[index]
    done_ref[own] = piece
    for index in range(PIECES - 1):
        to_near(index).start()

    convolve(shifted_grad, backward_ref, False, mask_ref, grad_ref, 2, 4)
    for index in range(PIECES - 1):
        to_near(index).wait()
    mine = chunk(half(full_ref, core), place)
    mine[...] = jnp.concatenate([done_ref[piece] for piece in range(PIECES)], axis=1)
    spread(PLANE - 1, to_all)
    settle(PLANE - 1, to_all)
    back_to_sibling.start()
    back_to_sibling.wait()
    cells = lax.axis_size("slab") * lax.axis_size("sub") * ROWS * ROWS * BRICK
    result_ref[...] = full_ref[:, : TAPS * C] * cells ** (-0.5)


def scratch():
    bf16, f32, dma = jnp.bfloat16, jnp.float32, pltpu.SemaphoreType.DMA
    return [
        pltpu.VMEM((ROWS, ROWS, XC), bf16),
        pltpu.VMEM((ROWS, ROWS, XC), bf16),
        pltpu.VMEM((C, TAPS * C), bf16),
        pltpu.SMEM((ROWS // BRICK, ROWS // BRICK), jnp.int32),
        pltpu.VMEM((ROWS // BRICK, ROWS, XC), f32),
        pltpu.VMEM((ROWS // BRICK, ROWS, XC), bf16),
        pltpu.VMEM((ROWS + 2, 48, PADX), f32),
        pltpu.VMEM((ROWS + 2, 48, PADX), f32),
        pltpu.VMEM((2, ROWS, XC), f32),
        pltpu.VMEM((2, ROWS, XC), f32),
        pltpu.VMEM((2, 48, PADX), f32),
        pltpu.VMEM((3, (ROWS + 2) * ROWS, PADX), bf16),
        pltpu.VMEM((3, (ROWS + 2) * ROWS, PADX), bf16),
        pltpu.VMEM((3, 128, 128 * (ROWS + 2)), bf16),
        pltpu.VMEM((2, 128, 128), bf16),
        pltpu.VMEM((256, 9 * WINDOW), bf16),
        pltpu.VMEM((9 * WINDOW, 256), bf16),
        pltpu.VMEM((3, 384, 256), f32),
        pltpu.VMEM((C, WIDE), f32),
        pltpu.VMEM((2, 2, ROWS, XC), bf16),
        pltpu.VMEM((2, 2, ROWS, XC), bf16),
        pltpu.VMEM((2, 2, ROWS, XC), bf16),
        pltpu.VMEM((2, 2, ROWS, XC), bf16),
        pltpu.VMEM((4, 8, XC), f32),
        pltpu.VMEM((4, 8, XC), f32),
        pltpu.VMEM((HALF, WIDE), f32),
        pltpu.VMEM((HALF, WIDE), f32),
        pltpu.VMEM((PLANE - 1, 8, CHUNK), f32),
        pltpu.VMEM((PIECES, 8, 128), f32),
        pltpu.VMEM((DEEP, 8, 128), f32),
        pltpu.VMEM((PIECES, 8, 128), f32),
        pltpu.VMEM((C, WIDE), f32),
        dma((4,)),
        dma((8,)),
        dma((8,)),
        dma((4,)),
        dma((PLANE - 1,)),
        dma((PLANE - 1,)),
        dma((DEEP - 1,)),
        dma((DEEP - 1,)),
        dma((PIECES - 1,)),
        dma((PIECES - 1,)),
        dma((PLANE - 1,)),
        dma((PLANE - 1,)),
    ]


def deliver_kernel(*refs):
    sources, targets, semaphores = refs[:3], refs[3:6], refs[6]
    copies = [
        pltpu.make_async_copy(source, target, semaphores.at[index])
        for index, (source, target) in enumerate(zip(sources, targets))
    ]
    for copy in copies:
        copy.start()
    for copy in copies:
        copy.wait()


def deliver(*arrays):
    return pl.pallas_call(
        deliver_kernel,
        out_shape=[jax.ShapeDtypeStruct(a.shape, a.dtype) for a in arrays],
        in_specs=[pl.BlockSpec(memory_space=pltpu.VMEM)] * 3,
        out_specs=[pl.BlockSpec(memory_space=pltpu.HBM)] * 3,
        scratch_shapes=[pltpu.SemaphoreType.DMA((3,))],
        compiler_params=pltpu.CompilerParams(vmem_limit_bytes=8 * 2**20),
        cost_estimate=pl.CostEstimate(
            flops=0, bytes_accessed=5 * 2**20, transcendentals=0
        ),
        name="deliver",
    )(*arrays)


def per_device(features, cotangent, weight, occupancy):
    hbm = pl.BlockSpec(memory_space=pltpu.HBM)
    out, grad, total = pl.pallas_call(
        kernel,
        out_shape=[
            pltpu.VMEM(features.shape, jnp.bfloat16),
            pltpu.VMEM(features.shape, jnp.bfloat16),
            pltpu.VMEM((C, TAPS * C), jnp.float32),
        ],
        in_specs=[hbm] * 4,
        out_specs=[pl.BlockSpec(memory_space=pltpu.VMEM)] * 3,
        scratch_shapes=scratch(),
        compiler_params=pltpu.CompilerParams(
            collective_id=0, has_side_effects=True, vmem_limit_bytes=55 * 2**20
        ),
        cost_estimate=pl.CostEstimate(
            flops=11 * 10**9, bytes_accessed=5 * 2**20, transcendentals=0
        ),
        name="convolutions",
    )(features, cotangent, weight, occupancy)
    return deliver(out, grad, total)


def solution(mesh):
    placed = (P("slab", "sub", None), P("slab", "sub", None), P(), P("slab", "sub"))
    return jax.shard_map(
        per_device,
        mesh=mesh,
        in_specs=placed,
        out_specs=(P("slab", "sub", None), P("slab", "sub", None), P()),
        check_vma=False,
    )
```

```python
import jax
import jax.numpy as jnp
from jax import lax
from jax.experimental import pallas as pl
from jax.experimental.pallas import tpu as pltpu
from jax.sharding import PartitionSpec as P

C = 64
BRICK = 8
ROWS = 32
XC = 512
PADX = XC + 2 * C
WINDOW = 384
TAPS = 27
MESH = pl.DeviceIdType.MESH
DEEP = 16
PLANE = 16
PIECES = 4
CHUNK = 512
WIDE = 4 * CHUNK
PLANE_STEPS = sorted(
    [(dy, dx) for dy in range(4) for dx in range(4) if dy or dx],
    key=lambda step: -min(step[0], 4 - step[0]) - min(step[1], 4 - step[1]),
)
COLUMN_STEPS = sorted(range(1, DEEP), key=lambda step: -min(step, DEEP - step))
NEAR_STEPS = (-2, -1, 1)
HALF = C // 2

FACES_Z = ((1, 0), (-1, 0))
FACES_Y = ((0, 1), (0, -1))
CORNERS = ((1, 1), (1, -1), (-1, 1), (-1, -1))
DIRECTIONS = FACES_Z + FACES_Y + CORNERS


def widen(rows):
    side = jnp.zeros(rows.shape[:-1] + (C,), rows.dtype)
    return jnp.concatenate([side, rows, side], axis=-1)


def pairs(rows):
    return jnp.concatenate([rows[:, 128 * p : 128 * p + 128] for p in range(4)], axis=0)


def pair_windows(rows):
    return jnp.concatenate([rows[:, 128 * p : 128 * p + 256] for p in range(4)], axis=0)


def build_masks(occ_ref, mask_ref, narrow_ref):
    row = lax.broadcasted_iota(jnp.int32, (ROWS, XC), 0) // BRICK
    for brick_z in range(ROWS // BRICK):
        mask = jnp.zeros((ROWS, XC), jnp.float32)
        for brick_y in range(ROWS // BRICK):
            flag = occ_ref[brick_z, brick_y].astype(jnp.float32)
            mask = jnp.where(row == brick_y, flag, mask)
        mask_ref[brick_z] = mask
        narrow_ref[brick_z] = mask.astype(jnp.bfloat16)


def build_weights(w_ref, forward_ref, backward_ref):
    for ab in range(9):
        taps = w_ref[:, 192 * ab : 192 * ab + 192]
        for x in range(4):
            parts = [taps]
            if x > 0:
                parts = [jnp.zeros((C, C * x), taps.dtype)] + parts
            if x < 3:
                parts = parts + [jnp.zeros((C, C * (3 - x)), taps.dtype)]
            forward_ref[C * x : C * x + C, WINDOW * ab : WINDOW * ab + WINDOW] = (
                jnp.concatenate(parts, axis=1)
            )
        mirrored = 8 - ab
        for x in range(6):
            low = C * (x - 2)
            first, last = max(0, -low), min(192, 256 - low)
            parts = [taps[:, first:last]]
            if low > 0:
                parts = [jnp.zeros((C, low), taps.dtype)] + parts
            end = low + last
            if end < 256:
                parts = parts + [jnp.zeros((C, 256 - end), taps.dtype)]
            start = WINDOW * mirrored + C * x
            backward_ref[start : start + C, :] = jnp.concatenate(parts, axis=1)


def clear_sides(stage_ref, turned_ref, share_ref):
    for side in range(2):
        stage_ref[side, 0:8, :] = jnp.zeros((8, PADX), jnp.float32)
        stage_ref[side, 40:48, :] = jnp.zeros((8, PADX), jnp.float32)
    for b in range(3):
        turned_ref[b, :, :128] = jnp.zeros((128, 128), turned_ref.dtype)
        turned_ref[b, :, 128 * (ROWS + 1) :] = jnp.zeros((128, 128), turned_ref.dtype)
    share_ref[:, TAPS * C :] = jnp.zeros((C, WIDE - TAPS * C), jnp.float32)


def cut_faces(raw_refs, mask_ref, edge_refs, buffers):
    face_send, _, edge_send, _, corner_send, _ = buffers

    def layer(z, _):
        mask = mask_ref[z // BRICK]
        for tensor in range(2):
            for side, tile in enumerate((0, ROWS - 16)):
                rows = raw_refs[tensor][z, tile : tile + 16, :].astype(jnp.float32)
                row = 0 if side == 0 else 15
                edge_refs[tensor][side, pl.ds(z, 1), :] = (
                    rows[row : row + 1] * mask[tile + row : tile + row + 1]
                )
        return 0

    lax.fori_loop(0, ROWS, layer, 0, unroll=4)
    for side, z in enumerate((ROWS - 1, 0)):
        for tensor in range(2):
            face = raw_refs[tensor][z].astype(jnp.float32) * mask_ref[z // BRICK]
            face_send[side, tensor] = face.astype(jnp.bfloat16)
            edge_send[side, tensor] = edge_refs[tensor][1 - side].astype(jnp.bfloat16)
    for index, (dz, dy) in enumerate(CORNERS):
        z = ROWS - 1 if dz > 0 else 0
        y = 1 if dy > 0 else 0
        corner_send[index] = jnp.concatenate(
            [edge_refs[0][y, z : z + 1, :], edge_refs[1][y, z : z + 1, :]]
            + [jnp.zeros((6, XC), jnp.float32)],
            axis=0,
        )


def prepare(raw_ref, narrow_ref, shifted_ref, unroll=8):
    def layer(z, _):
        rows = pl.ds(pl.multiple_of((z + 1) * ROWS, ROWS), ROWS)
        shifted_ref[1, rows, :] = widen(raw_ref[z] * narrow_ref[z // BRICK])
        return 0

    lax.fori_loop(0, ROWS, layer, 0, unroll=unroll)


def prepare_both(features_ref, cotangent_ref, narrow_ref, shifted_ref, turned_ref):
    edge = jnp.zeros((128, 1), jnp.bfloat16)
    row = lax.broadcasted_iota(jnp.int32, (128, 128), 1) % ROWS
    not_last = (row != ROWS - 1).astype(jnp.float32).astype(jnp.bfloat16)
    not_first = (row != 0).astype(jnp.float32).astype(jnp.bfloat16)

    def layer(z, _):
        mask = narrow_ref[z // BRICK]
        rows = pl.ds(pl.multiple_of((z + 1) * ROWS, ROWS), ROWS)
        shifted_ref[1, rows, :] = widen(features_ref[z] * mask)
        column = pl.ds(pl.multiple_of(128 * (z + 1), 128), 128)
        turned = pairs(cotangent_ref[z] * mask).T
        turned_ref[0, :, column] = not_last * jnp.concatenate([turned[:, 1:], edge], axis=1)
        turned_ref[1, :, column] = turned
        turned_ref[2, :, column] = not_first * jnp.concatenate([edge, turned[:, :127]], axis=1)
        return 0

    lax.fori_loop(0, ROWS, layer, 0, unroll=8)


def pad_rows(shifted_ref, padded_ref):
    def layer(z, _):
        rows = pl.ds(pl.multiple_of((z + 1) * ROWS, ROWS), ROWS)
        padded_ref[z + 1, 8:40, :] = shifted_ref[1, rows, :].astype(jnp.float32)
        return 0

    lax.fori_loop(0, ROWS, layer, 0, unroll=4)


def shift_layer(padded_ref, shifted_ref, z, shifts):
    rows = pl.ds(pl.multiple_of(z * ROWS, ROWS), ROWS)
    for b in shifts:
        shifted_ref[b, rows, :] = padded_ref[z, 7 + b : 39 + b, :].astype(jnp.bfloat16)


def shift_rows(padded_ref, shifted_ref):
    def layer(z, _):
        shift_layer(padded_ref, shifted_ref, z, (0, 2))
        return 0

    lax.fori_loop(1, ROWS + 1, layer, 0, unroll=8)


def inner_gradient(turned_ref, shifted_ref, product_ref):
    window = jnp.concatenate(
        [
            shifted_ref[1, ROWS * z : ROWS * z + ROWS, 128 * p : 128 * p + 256]
            for z in range(1, ROWS + 1)
            for p in range(4)
        ],
        axis=0,
    )
    for b in range(3):
        turned = jnp.concatenate(
            [turned_ref[b, :, 128 * (2 - a) : 128 * (2 - a + ROWS)] for a in range(3)],
            axis=0,
        )
        product_ref[b] = jnp.dot(turned, window, preferred_element_type=jnp.float32)


def outer_gradient(turned_ref, shifted_ref, edge_turned_ref, stage_ref, product_ref, share_ref):
    def along_z(z, layer):
        first = ROWS * layer
        window = jnp.concatenate(
            [pair_windows(shifted_ref[b, first : first + ROWS, :]) for b in range(3)],
            axis=1,
        )
        column = turned_ref[1, :, 128 * (z + 1) : 128 * (z + 2)]
        return jnp.dot(column, window, preferred_element_type=jnp.float32)

    def along_y(side):
        window = jnp.concatenate(
            [
                pair_windows(stage_ref[side, 7 + a : 39 + a, :].astype(jnp.bfloat16))
                for a in range(3)
            ],
            axis=1,
        )
        return jnp.dot(edge_turned_ref[side], window, preferred_element_type=jnp.float32)

    low_z, high_z = along_z(0, 0), along_z(ROWS - 1, ROWS + 1)
    edges = {0: along_y(0), 2: along_y(1)}
    for b in range(3):
        for a in range(3):
            term = product_ref[b, 128 * a : 128 * a + 128, :]
            if a == 0:
                term = term + low_z[:, 256 * b : 256 * b + 256]
            if a == 2:
                term = term + high_z[:, 256 * b : 256 * b + 256]
            if b != 1:
                term = term + edges[b][:, 256 * a : 256 * a + 256]
            ab = 3 * a + b
            share_ref[:, 192 * ab : 192 * ab + 192] = (
                term[:C, :192] + term[C:, C : C + 192]
            )


def convolve(shifted_ref, weight_ref, transposed, mask_ref, out_ref, start, stop, layers=BRICK):
    contract = (((1,), (1 if transposed else 0,)), ((), ()))

    def block(step, _):
        first = step * layers
        mask = mask_ref[first // BRICK, :, :256]
        for quad in range(2):
            window = jnp.concatenate(
                [
                    shifted_ref[
                        b,
                        pl.ds(pl.multiple_of((first + a) * ROWS, ROWS), layers * ROWS),
                        256 * quad : 256 * quad + WINDOW,
                    ]
                    for a in range(3)
                    for b in range(3)
                ],
                axis=1,
            )
            total = lax.dot_general(
                window, weight_ref[...], contract, preferred_element_type=jnp.float32
            )
            total = total.reshape(layers, ROWS, 256) * mask[None]
            out_ref[pl.ds(first, layers), :, 256 * quad : 256 * quad + 256] = total.astype(
                jnp.bfloat16
            )
        return 0

    lax.fori_loop(start, stop, block, 0)


def neighbour(direction):
    slabs, subs = lax.axis_size("slab"), lax.axis_size("sub")
    slab = lax.rem(lax.axis_index("slab") + direction[0] + slabs, slabs)
    sub = lax.rem(lax.axis_index("sub") + direction[1] + subs, subs)
    return slab, sub


def within(direction):
    dz, dy = direction
    inside = jnp.int32(1)
    if dz:
        edge = 0 if dz > 0 else lax.axis_size("slab") - 1
        inside = inside * jnp.where(lax.axis_index("slab") == edge, 0, 1)
    if dy:
        edge = 0 if dy > 0 else lax.axis_size("sub") - 1
        inside = inside * jnp.where(lax.axis_index("sub") == edge, 0, 1)
    return inside.astype(jnp.float32)


def halo_copies(buffers, send_sem, recv_sem):
    face_send, face_recv, edge_send, edge_recv, corner_send, corner_recv = buffers
    copies = []
    for index, direction in enumerate(DIRECTIONS):
        if index < 2:
            source, target = face_send.at[index], face_recv.at[index]
        elif index < 4:
            source, target = edge_send.at[index - 2], edge_recv.at[index - 2]
        else:
            source, target = corner_send.at[index - 4], corner_recv.at[index - 4]
        copies.append(
            pltpu.make_async_remote_copy(
                src_ref=source,
                dst_ref=target,
                send_sem=send_sem.at[index],
                recv_sem=recv_sem.at[index],
                device_id=neighbour(direction),
                device_id_type=MESH,
            )
        )
    return copies


def place_layers(tensor, buffers, padded_ref):
    _, face_recv, _, _, _, corner_recv = buffers
    for index, direction in enumerate(FACES_Z):
        layer = 0 if index == 0 else ROWS + 1
        face = face_recv[index, tensor].astype(jnp.float32) * within(direction)
        padded_ref[layer, 8:40, :] = widen(face)
    for index, direction in enumerate(CORNERS):
        layer = 0 if direction[0] > 0 else ROWS + 1
        row = 7 if direction[1] > 0 else 40
        corner = corner_recv[index, tensor : tensor + 1, :] * within(direction)
        padded_ref[layer, row : row + 1, :] = widen(corner)


def stage_edges(tensor, buffers, stage_ref):
    _, _, _, edge_recv, _, _ = buffers
    for index, direction in enumerate(FACES_Y):
        edge = edge_recv[index, tensor].astype(jnp.float32) * within(direction)
        stage_ref[index, 8:40, :] = widen(edge)


def place_rows(stage_ref, padded_ref):
    def layer(z, _):
        for side, row in enumerate((7, 40)):
            padded_ref[z + 1, row : row + 1, :] = stage_ref[side, pl.ds(8 + z, 1), :]
        return 0

    lax.fori_loop(0, ROWS, layer, 0)


def start(copies):
    for copy in copies:
        copy.start()


def arrived(same_bytes, semaphores):
    pltpu.make_async_copy(same_bytes, same_bytes, semaphores.at[1]).wait()


def left(same_bytes, semaphores):
    pltpu.make_async_copy(same_bytes, same_bytes, semaphores.at[0]).wait()


def sibling():
    slab = lax.axis_index("slab")
    return slab + 1 - 2 * lax.rem(slab, 2), lax.axis_index("sub")


def plane_place():
    return lax.rem(lax.axis_index("slab") // 2, 4) * 4 + lax.axis_index("sub")


def plane_partner(step):
    slab, sub = lax.axis_index("slab"), lax.axis_index("sub")
    y, x = lax.rem(slab // 2 + step[0], 4), lax.rem(sub + step[1], 4)
    return (slab // 8 * 8 + y * 2 + lax.rem(slab, 2), x), y * 4 + x


def column_partner(step):
    slab = lax.axis_index("slab")
    z = lax.rem(slab // 8 + step + DEEP, DEEP)
    return (z * 8 + lax.rem(slab, 8), lax.axis_index("sub")), z


def chunk(ref, place):
    row = pl.multiple_of(place // 4 * 8, 8)
    lane = pl.multiple_of(lax.rem(place, 4) * CHUNK, CHUNK)
    return ref.at[pl.ds(row, 8), pl.ds(lane, CHUNK)]


def half(ref, core):
    return ref.at[pl.ds(pl.multiple_of(core * HALF, HALF), HALF)]


def greet():
    semaphore = pltpu.get_barrier_semaphore()

    def signal(device):
        pl.semaphore_signal(semaphore, inc=1, device_id=device, device_id_type=MESH)

    for direction in DIRECTIONS:
        signal(neighbour(direction))
    signal(sibling())
    for step in PLANE_STEPS:
        signal(plane_partner(step)[0])
    for step in (1, -1):
        signal(column_partner(step)[0])
    return lambda: pl.semaphore_wait(
        semaphore, len(DIRECTIONS) + 1 + len(PLANE_STEPS) + 2
    )


def tell(round_sem, index):
    for step in (2**index, -(2**index)):
        pl.semaphore_signal(
            round_sem.at[index],
            inc=1,
            device_id=column_partner(step)[0],
            device_id_type=MESH,
        )


def hear(round_sem, index):
    pl.semaphore_wait(round_sem.at[index], 2)


def kernel(
    features_hbm,
    cotangent_hbm,
    weight_hbm,
    occ_hbm,
    out_ref,
    grad_ref,
    result_ref,
    features_ref,
    cotangent_ref,
    weight_ref,
    occ_ref,
    mask_ref,
    narrow_ref,
    padded_in,
    padded_grad,
    edge_in,
    edge_grad,
    stage_ref,
    shifted_in,
    shifted_grad,
    turned_ref,
    edge_turned_ref,
    forward_ref,
    backward_ref,
    product_ref,
    share_ref,
    face_send,
    face_recv,
    edge_send,
    edge_recv,
    corner_send,
    corner_recv,
    core_recv,
    half_ref,
    plane_recv,
    pieces_ref,
    column_recv,
    done_ref,
    full_ref,
    load_sem,
    halo_send_sem,
    halo_recv_sem,
    core_sem,
    plane_sem,
    column_sem,
    near_sem,
    gather_sem,
    round_sem,
):
    loads = [
        pltpu.make_async_copy(features_hbm, features_ref, load_sem.at[0]),
        pltpu.make_async_copy(cotangent_hbm, cotangent_ref, load_sem.at[1]),
        pltpu.make_async_copy(weight_hbm, weight_ref, load_sem.at[2]),
    ]
    flags = pltpu.make_async_copy(occ_hbm, occ_ref, load_sem.at[3])
    slab = lax.axis_index("slab")
    z, core, place = slab // 8, lax.rem(slab, 2), plane_place()
    own = lax.rem(z, PIECES)
    buffers = (face_send, face_recv, edge_send, edge_recv, corner_send, corner_recv)
    halos = halo_copies(buffers, halo_send_sem, halo_recv_sem)
    to_sibling = pltpu.make_async_remote_copy(
        src_ref=half(share_ref, 1 - core),
        dst_ref=core_recv,
        send_sem=core_sem.at[0],
        recv_sem=core_sem.at[1],
        device_id=sibling(),
        device_id_type=MESH,
    )

    mine = chunk(half(full_ref, core), place)
    to_plane, to_all = [], []
    for index, step in enumerate(PLANE_STEPS):
        device, other = plane_partner(step)
        to_plane.append(
            pltpu.make_async_remote_copy(
                src_ref=chunk(half_ref, other),
                dst_ref=plane_recv.at[index],
                send_sem=plane_sem.at[0],
                recv_sem=plane_sem.at[1],
                device_id=device,
                device_id_type=MESH,
            )
        )
        to_all.append(
            pltpu.make_async_remote_copy(
                src_ref=mine,
                dst_ref=mine,
                send_sem=gather_sem.at[0],
                recv_sem=gather_sem.at[1],
                device_id=device,
                device_id_type=MESH,
            )
        )
    to_column = []
    for step in COLUMN_STEPS:
        device, other = column_partner(step)
        to_column.append(
            pltpu.make_async_remote_copy(
                src_ref=pieces_ref.at[lax.rem(other, PIECES)],
                dst_ref=column_recv.at[z],
                send_sem=column_sem.at[0],
                recv_sem=column_sem.at[1],
                device_id=device,
                device_id_type=MESH,
            )
        )
    to_near = [
        pltpu.make_async_remote_copy(
            src_ref=done_ref.at[own],
            dst_ref=done_ref.at[own],
            send_sem=near_sem.at[0],
            recv_sem=near_sem.at[1],
            device_id=column_partner(step)[0],
            device_id_type=MESH,
        )
        for step in NEAR_STEPS
    ]
    column_bytes = column_recv.at[pl.ds(0, DEEP - 1)]
    near_bytes = done_ref.at[pl.ds(0, PIECES - 1)]

    back_to_sibling = pltpu.make_async_remote_copy(
        src_ref=half(full_ref, core),
        dst_ref=half(full_ref, core),
        send_sem=core_sem.at[2],
        recv_sem=core_sem.at[3],
        device_id=sibling(),
        device_id_type=MESH,
    )

    flags.start()
    for load in loads:
        load.start()
    everyone_here = greet()
    clear_sides(stage_ref, turned_ref, share_ref)
    flags.wait()
    build_masks(occ_ref, mask_ref, narrow_ref)
    for load in loads:
        load.wait()
    cut_faces((features_ref, cotangent_ref), mask_ref, (edge_in, edge_grad), buffers)
    everyone_here()
    for copy in halos:
        copy.start()
    tell(round_sem, 0)

    prepare_both(features_ref, cotangent_ref, narrow_ref, shifted_in, turned_ref)
    for side in range(2):
        edge_turned_ref[side] = pairs(edge_grad[side]).T.astype(jnp.bfloat16)
    inner_gradient(turned_ref, shifted_in, product_ref)

    hear(round_sem, 0)
    tell(round_sem, 1)
    for copy in halos:
        copy.wait()
    place_layers(0, buffers, padded_in)
    for layer in (0, ROWS + 1):
        shift_layer(padded_in, shifted_in, layer, (0, 1, 2))
    stage_edges(0, buffers, stage_ref)
    outer_gradient(
        turned_ref, shifted_in, edge_turned_ref, stage_ref, product_ref, share_ref
    )
    to_sibling.start()

    build_weights(weight_ref, forward_ref, backward_ref)
    pad_rows(shifted_in, padded_in)
    to_sibling.wait()
    hear(round_sem, 1)
    tell(round_sem, 2)
    half_ref[...] = half(share_ref, core)[...] + core_recv[...]
    start(to_plane)

    place_rows(stage_ref, padded_in)
    shift_rows(padded_in, shifted_in)
    convolve(shifted_in, forward_ref, True, mask_ref, out_ref, 0, 3)
    arrived(plane_recv, plane_sem)
    total = chunk(half_ref, place)[...]
    for index in range(PLANE - 1):
        total = total + plane_recv[index]
    for piece in range(PIECES):
        pieces_ref[piece] = total[:, 128 * piece : 128 * piece + 128]
    hear(round_sem, 2)
    start(to_column)

    convolve(shifted_in, forward_ref, True, mask_ref, out_ref, 3, 4)
    prepare(cotangent_ref, narrow_ref, shifted_grad)
    pad_rows(shifted_grad, padded_grad)
    place_layers(1, buffers, padded_grad)
    stage_edges(1, buffers, stage_ref)
    place_rows(stage_ref, padded_grad)
    shift_rows(padded_grad, shifted_grad)
    for layer in (0, ROWS + 1):
        shift_layer(padded_grad, shifted_grad, layer, (0, 1, 2))
    convolve(shifted_grad, backward_ref, False, mask_ref, grad_ref, 0, 2)
    arrived(column_bytes, column_sem)
    column_recv[z] = pieces_ref[own]
    piece = column_recv[0]
    for index in range(1, DEEP):
        piece = piece + column_recv[index]
    done_ref[own] = piece
    start(to_near)

    convolve(shifted_grad, backward_ref, False, mask_ref, grad_ref, 2, 4)
    arrived(near_bytes, near_sem)
    mine[...] = jnp.concatenate([done_ref[piece] for piece in range(PIECES)], axis=1)
    start(to_all)
    arrived(plane_recv, gather_sem)
    back_to_sibling.start()
    left(plane_recv, plane_sem)
    left(column_bytes, column_sem)
    left(near_bytes, near_sem)
    left(plane_recv, gather_sem)
    back_to_sibling.wait()
    cells = lax.axis_size("slab") * lax.axis_size("sub") * ROWS * ROWS * BRICK
    result_ref[...] = full_ref[:, : TAPS * C] * cells ** (-0.5)


def scratch():
    bf16, f32, dma = jnp.bfloat16, jnp.float32, pltpu.SemaphoreType.DMA
    return [
        pltpu.VMEM((ROWS, ROWS, XC), bf16),
        pltpu.VMEM((ROWS, ROWS, XC), bf16),
        pltpu.VMEM((C, TAPS * C), bf16),
        pltpu.SMEM((ROWS // BRICK, ROWS // BRICK), jnp.int32),
        pltpu.VMEM((ROWS // BRICK, ROWS, XC), f32),
        pltpu.VMEM((ROWS // BRICK, ROWS, XC), bf16),
        pltpu.VMEM((ROWS + 2, 48, PADX), f32),
        pltpu.VMEM((ROWS + 2, 48, PADX), f32),
        pltpu.VMEM((2, ROWS, XC), f32),
        pltpu.VMEM((2, ROWS, XC), f32),
        pltpu.VMEM((2, 48, PADX), f32),
        pltpu.VMEM((3, (ROWS + 2) * ROWS, PADX), bf16),
        pltpu.VMEM((3, (ROWS + 2) * ROWS, PADX), bf16),
        pltpu.VMEM((3, 128, 128 * (ROWS + 2)), bf16),
        pltpu.VMEM((2, 128, 128), bf16),
        pltpu.VMEM((256, 9 * WINDOW), bf16),
        pltpu.VMEM((9 * WINDOW, 256), bf16),
        pltpu.VMEM((3, 384, 256), f32),
        pltpu.VMEM((C, WIDE), f32),
        pltpu.VMEM((2, 2, ROWS, XC), bf16),
        pltpu.VMEM((2, 2, ROWS, XC), bf16),
        pltpu.VMEM((2, 2, ROWS, XC), bf16),
        pltpu.VMEM((2, 2, ROWS, XC), bf16),
        pltpu.VMEM((4, 8, XC), f32),
        pltpu.VMEM((4, 8, XC), f32),
        pltpu.VMEM((HALF, WIDE), f32),
        pltpu.VMEM((HALF, WIDE), f32),
        pltpu.VMEM((PLANE - 1, 8, CHUNK), f32),
        pltpu.VMEM((PIECES, 8, 128), f32),
        pltpu.VMEM((DEEP, 8, 128), f32),
        pltpu.VMEM((PIECES, 8, 128), f32),
        pltpu.VMEM((C, WIDE), f32),
        dma((4,)),
        dma((8,)),
        dma((8,)),
        dma((4,)),
        dma((2,)),
        dma((2,)),
        dma((2,)),
        dma((2,)),
        pltpu.SemaphoreType.REGULAR((3,)),
    ]


def deliver_kernel(*refs):
    sources, targets, semaphores = refs[:3], refs[3:6], refs[6]
    copies = [
        pltpu.make_async_copy(source, target, semaphores.at[index])
        for index, (source, target) in enumerate(zip(sources, targets))
    ]
    for copy in copies:
        copy.start()
    for copy in copies:
        copy.wait()


def deliver(*arrays):
    return pl.pallas_call(
        deliver_kernel,
        out_shape=[jax.ShapeDtypeStruct(a.shape, a.dtype) for a in arrays],
        in_specs=[pl.BlockSpec(memory_space=pltpu.VMEM)] * 3,
        out_specs=[pl.BlockSpec(memory_space=pltpu.HBM)] * 3,
        scratch_shapes=[pltpu.SemaphoreType.DMA((3,))],
        compiler_params=pltpu.CompilerParams(vmem_limit_bytes=8 * 2**20),
        cost_estimate=pl.CostEstimate(
            flops=0, bytes_accessed=5 * 2**20, transcendentals=0
        ),
        name="deliver",
    )(*arrays)


def per_device(features, cotangent, weight, occupancy):
    hbm = pl.BlockSpec(memory_space=pltpu.HBM)
    out, grad, total = pl.pallas_call(
        kernel,
        out_shape=[
            pltpu.VMEM(features.shape, jnp.bfloat16),
            pltpu.VMEM(features.shape, jnp.bfloat16),
            pltpu.VMEM((C, TAPS * C), jnp.float32),
        ],
        in_specs=[hbm] * 4,
        out_specs=[pl.BlockSpec(memory_space=pltpu.VMEM)] * 3,
        scratch_shapes=scratch(),
        compiler_params=pltpu.CompilerParams(
            collective_id=0, has_side_effects=True, vmem_limit_bytes=55 * 2**20
        ),
        cost_estimate=pl.CostEstimate(
            flops=11 * 10**9, bytes_accessed=5 * 2**20, transcendentals=0
        ),
        name="convolutions",
    )(features, cotangent, weight, occupancy)
    return deliver(out, grad, total)


def solution(mesh):
    placed = (P("slab", "sub", None), P("slab", "sub", None), P(), P("slab", "sub"))
    return jax.shard_map(
        per_device,
        mesh=mesh,
        in_specs=placed,
        out_specs=(P("slab", "sub", None), P("slab", "sub", None), P()),
        check_vma=False,
    )
```

```python
import jax
import jax.numpy as jnp
from jax import lax
from jax.experimental import pallas as pl
from jax.experimental.pallas import tpu as pltpu
from jax.sharding import PartitionSpec as P

C = 64
BRICK = 8
ROWS = 32
XC = 512
PADX = XC + 2 * C
WINDOW = 384
TAPS = 27
MESH = pl.DeviceIdType.MESH
DEEP = 16
PLANE = 16
PIECES = 4
CHUNK = 512
WIDE = 4 * CHUNK
PLANE_STEPS = sorted(
    [(dy, dx) for dy in range(4) for dx in range(4) if dy or dx],
    key=lambda step: -min(step[0], 4 - step[0]) - min(step[1], 4 - step[1]),
)
PLANE_ROUNDS = (((0, 1), (0, 3), (1, 0), (3, 0)), ((1, 1), (1, 3), (3, 1), (3, 3)))
COLUMN_STEPS = sorted(range(1, DEEP), key=lambda step: -min(step, DEEP - step))
NEAR_STEPS = sorted(
    [
        (dz, dy, dx)
        for dz in (-2, -1, 0, 1)
        for dy in range(4)
        for dx in range(4)
        if dz or dy or dx
    ],
    key=lambda step: -abs(step[0]) - min(step[1], 4 - step[1]) - min(step[2], 4 - step[2]),
)
HALF = C // 2

FACES_Z = ((1, 0), (-1, 0))
FACES_Y = ((0, 1), (0, -1))
CORNERS = ((1, 1), (1, -1), (-1, 1), (-1, -1))
DIRECTIONS = FACES_Z + FACES_Y + CORNERS


def widen(rows):
    side = jnp.zeros(rows.shape[:-1] + (C,), rows.dtype)
    return jnp.concatenate([side, rows, side], axis=-1)


def pairs(rows):
    return jnp.concatenate([rows[:, 128 * p : 128 * p + 128] for p in range(4)], axis=0)


def pair_windows(rows):
    return jnp.concatenate([rows[:, 128 * p : 128 * p + 256] for p in range(4)], axis=0)


def build_masks(occ_ref, mask_ref, narrow_ref):
    row = lax.broadcasted_iota(jnp.int32, (ROWS, XC), 0) // BRICK
    for brick_z in range(ROWS // BRICK):
        mask = jnp.zeros((ROWS, XC), jnp.float32)
        for brick_y in range(ROWS // BRICK):
            flag = occ_ref[brick_z, brick_y].astype(jnp.float32)
            mask = jnp.where(row == brick_y, flag, mask)
        mask_ref[brick_z] = mask
        narrow_ref[brick_z] = mask.astype(jnp.bfloat16)


def build_weights(w_ref, forward_ref, backward_ref):
    for ab in range(9):
        taps = w_ref[:, 192 * ab : 192 * ab + 192]
        for x in range(4):
            parts = [taps]
            if x > 0:
                parts = [jnp.zeros((C, C * x), taps.dtype)] + parts
            if x < 3:
                parts = parts + [jnp.zeros((C, C * (3 - x)), taps.dtype)]
            forward_ref[C * x : C * x + C, WINDOW * ab : WINDOW * ab + WINDOW] = (
                jnp.concatenate(parts, axis=1)
            )
        mirrored = 8 - ab
        for x in range(6):
            low = C * (x - 2)
            first, last = max(0, -low), min(192, 256 - low)
            parts = [taps[:, first:last]]
            if low > 0:
                parts = [jnp.zeros((C, low), taps.dtype)] + parts
            end = low + last
            if end < 256:
                parts = parts + [jnp.zeros((C, 256 - end), taps.dtype)]
            start = WINDOW * mirrored + C * x
            backward_ref[start : start + C, :] = jnp.concatenate(parts, axis=1)


def clear_sides(stage_ref, turned_ref, share_ref):
    for side in range(2):
        stage_ref[side, 0:8, :] = jnp.zeros((8, PADX), jnp.float32)
        stage_ref[side, 40:48, :] = jnp.zeros((8, PADX), jnp.float32)
    for b in range(3):
        turned_ref[b, :, :128] = jnp.zeros((128, 128), turned_ref.dtype)
        turned_ref[b, :, 128 * (ROWS + 1) :] = jnp.zeros((128, 128), turned_ref.dtype)
    share_ref[:, TAPS * C :] = jnp.zeros((C, WIDE - TAPS * C), jnp.float32)


def cut_faces(raw_refs, mask_ref, edge_refs, buffers):
    face_send, _, edge_send, _, corner_send, _ = buffers

    def layer(z, _):
        mask = mask_ref[z // BRICK]
        for tensor in range(2):
            for side, tile in enumerate((0, ROWS - 16)):
                rows = raw_refs[tensor][z, tile : tile + 16, :].astype(jnp.float32)
                row = 0 if side == 0 else 15
                edge_refs[tensor][side, pl.ds(z, 1), :] = (
                    rows[row : row + 1] * mask[tile + row : tile + row + 1]
                )
        return 0

    lax.fori_loop(0, ROWS, layer, 0, unroll=4)
    for side, z in enumerate((ROWS - 1, 0)):
        for tensor in range(2):
            face = raw_refs[tensor][z].astype(jnp.float32) * mask_ref[z // BRICK]
            face_send[side, tensor] = face.astype(jnp.bfloat16)
            edge_send[side, tensor] = edge_refs[tensor][1 - side].astype(jnp.bfloat16)
    for index, (dz, dy) in enumerate(CORNERS):
        z = ROWS - 1 if dz > 0 else 0
        y = 1 if dy > 0 else 0
        corner_send[index] = jnp.concatenate(
            [edge_refs[0][y, z : z + 1, :], edge_refs[1][y, z : z + 1, :]]
            + [jnp.zeros((6, XC), jnp.float32)],
            axis=0,
        )


def prepare(raw_ref, narrow_ref, shifted_ref, unroll=8):
    def layer(z, _):
        rows = pl.ds(pl.multiple_of((z + 1) * ROWS, ROWS), ROWS)
        shifted_ref[1, rows, :] = widen(raw_ref[z] * narrow_ref[z // BRICK])
        return 0

    lax.fori_loop(0, ROWS, layer, 0, unroll=unroll)


def prepare_both(features_ref, cotangent_ref, narrow_ref, shifted_ref, turned_ref, layers):
    edge = jnp.zeros((128, 1), jnp.bfloat16)
    row = lax.broadcasted_iota(jnp.int32, (128, 128), 1) % ROWS
    not_last = (row != ROWS - 1).astype(jnp.float32).astype(jnp.bfloat16)
    not_first = (row != 0).astype(jnp.float32).astype(jnp.bfloat16)
    for z in layers:
        mask = narrow_ref[z // BRICK]
        shifted_ref[1, ROWS * (z + 1) : ROWS * (z + 2), :] = widen(features_ref[z] * mask)
        column = slice(128 * (z + 1), 128 * (z + 2))
        turned = pairs(cotangent_ref[z] * mask).T
        down = jnp.concatenate([turned[:, 1:], edge], axis=1)
        up = jnp.concatenate([edge, turned[:, :127]], axis=1)
        turned_ref[0, :, column] = not_last * down
        turned_ref[1, :, column] = turned
        turned_ref[2, :, column] = not_first * up


def pad_rows(shifted_ref, padded_ref):
    def layer(z, _):
        rows = pl.ds(pl.multiple_of((z + 1) * ROWS, ROWS), ROWS)
        padded_ref[z + 1, 8:40, :] = shifted_ref[1, rows, :].astype(jnp.float32)
        return 0

    lax.fori_loop(0, ROWS, layer, 0, unroll=4)


def shift_layer(padded_ref, shifted_ref, z, shifts):
    rows = pl.ds(pl.multiple_of(z * ROWS, ROWS), ROWS)
    for b in shifts:
        shifted_ref[b, rows, :] = padded_ref[z, 7 + b : 39 + b, :].astype(jnp.bfloat16)


def shift_rows(padded_ref, shifted_ref):
    def layer(z, _):
        shift_layer(padded_ref, shifted_ref, z, (0, 2))
        return 0

    lax.fori_loop(1, ROWS + 1, layer, 0, unroll=8)


def inner_gradient(turned_ref, shifted_ref, product_ref, first, last):
    window = jnp.concatenate(
        [
            shifted_ref[1, ROWS * z : ROWS * z + ROWS, 128 * p : 128 * p + 256]
            for z in range(first + 1, last + 1)
            for p in range(4)
        ],
        axis=0,
    )
    for b in range(3):
        turned = jnp.concatenate(
            [
                turned_ref[b, :, 128 * (first + 2 - a) : 128 * (last + 2 - a)]
                for a in range(3)
            ],
            axis=0,
        )
        product = jnp.dot(turned, window, preferred_element_type=jnp.float32)
        if first > 0:
            product = product_ref[b] + product
        product_ref[b] = product


def outer_gradient(turned_ref, shifted_ref, edge_turned_ref, stage_ref, product_ref, share_ref, done):
    def along_z(z, layer):
        first = ROWS * layer
        window = jnp.concatenate(
            [pair_windows(shifted_ref[b, first : first + ROWS, :]) for b in range(3)],
            axis=1,
        )
        column = turned_ref[1, :, 128 * (z + 1) : 128 * (z + 2)]
        return jnp.dot(column, window, preferred_element_type=jnp.float32)

    def along_y(side):
        window = jnp.concatenate(
            [
                pair_windows(stage_ref[side, 7 + a : 39 + a, :].astype(jnp.bfloat16))
                for a in range(3)
            ],
            axis=1,
        )
        return jnp.dot(edge_turned_ref[side], window, preferred_element_type=jnp.float32)

    low_z, high_z = along_z(0, 0), along_z(ROWS - 1, ROWS + 1)
    edges = {0: along_y(0), 2: along_y(1)}
    for a in range(3):
        for b in range(3):
            term = product_ref[b, 128 * a : 128 * a + 128, :]
            if a == 0:
                term = term + low_z[:, 256 * b : 256 * b + 256]
            if a == 2:
                term = term + high_z[:, 256 * b : 256 * b + 256]
            if b != 1:
                term = term + edges[b][:, 256 * a : 256 * a + 256]
            ab = 3 * a + b
            share_ref[:, 192 * ab : 192 * ab + 192] = (
                term[:C, :192] + term[C:, C : C + 192]
            )
        done(a)


def convolve(shifted_ref, weight_ref, transposed, mask_ref, out_ref, start, stop, layers=BRICK):
    contract = (((1,), (1 if transposed else 0,)), ((), ()))

    def block(step, _):
        first = step * layers
        mask = mask_ref[first // BRICK, :, :256]
        for quad in range(2):
            window = jnp.concatenate(
                [
                    shifted_ref[
                        b,
                        pl.ds(pl.multiple_of((first + a) * ROWS, ROWS), layers * ROWS),
                        256 * quad : 256 * quad + WINDOW,
                    ]
                    for a in range(3)
                    for b in range(3)
                ],
                axis=1,
            )
            total = lax.dot_general(
                window, weight_ref[...], contract, preferred_element_type=jnp.float32
            )
            total = total.reshape(layers, ROWS, 256) * mask[None]
            out_ref[pl.ds(first, layers), :, 256 * quad : 256 * quad + 256] = total.astype(
                jnp.bfloat16
            )
        return 0

    lax.fori_loop(start, stop, block, 0)


def neighbour(direction):
    slabs, subs = lax.axis_size("slab"), lax.axis_size("sub")
    slab = lax.rem(lax.axis_index("slab") + direction[0] + slabs, slabs)
    sub = lax.rem(lax.axis_index("sub") + direction[1] + subs, subs)
    return slab, sub


def within(direction):
    dz, dy = direction
    inside = jnp.int32(1)
    if dz:
        edge = 0 if dz > 0 else lax.axis_size("slab") - 1
        inside = inside * jnp.where(lax.axis_index("slab") == edge, 0, 1)
    if dy:
        edge = 0 if dy > 0 else lax.axis_size("sub") - 1
        inside = inside * jnp.where(lax.axis_index("sub") == edge, 0, 1)
    return inside.astype(jnp.float32)


def halo_copies(buffers, send_sem, recv_sem):
    face_send, face_recv, edge_send, edge_recv, corner_send, corner_recv = buffers
    copies = []
    for index, direction in enumerate(DIRECTIONS):
        if index < 2:
            source, target = face_send.at[index], face_recv.at[index]
        elif index < 4:
            source, target = edge_send.at[index - 2], edge_recv.at[index - 2]
        else:
            source, target = corner_send.at[index - 4], corner_recv.at[index - 4]
        copies.append(
            pltpu.make_async_remote_copy(
                src_ref=source,
                dst_ref=target,
                send_sem=send_sem.at[index],
                recv_sem=recv_sem.at[index],
                device_id=neighbour(direction),
                device_id_type=MESH,
            )
        )
    return copies


def place_layers(tensor, buffers, padded_ref):
    _, face_recv, _, _, _, corner_recv = buffers
    for index, direction in enumerate(FACES_Z):
        layer = 0 if index == 0 else ROWS + 1
        face = face_recv[index, tensor].astype(jnp.float32) * within(direction)
        padded_ref[layer, 8:40, :] = widen(face)
    for index, direction in enumerate(CORNERS):
        layer = 0 if direction[0] > 0 else ROWS + 1
        row = 7 if direction[1] > 0 else 40
        corner = corner_recv[index, tensor : tensor + 1, :] * within(direction)
        padded_ref[layer, row : row + 1, :] = widen(corner)


def stage_edges(tensor, buffers, stage_ref):
    _, _, _, edge_recv, _, _ = buffers
    for index, direction in enumerate(FACES_Y):
        edge = edge_recv[index, tensor].astype(jnp.float32) * within(direction)
        stage_ref[index, 8:40, :] = widen(edge)


def place_rows(stage_ref, padded_ref):
    def layer(z, _):
        for side, row in enumerate((7, 40)):
            padded_ref[z + 1, row : row + 1, :] = stage_ref[side, pl.ds(8 + z, 1), :]
        return 0

    lax.fori_loop(0, ROWS, layer, 0)


def start(copies):
    for copy in copies:
        copy.start()


def arrived(same_bytes, semaphores):
    pltpu.make_async_copy(same_bytes, same_bytes, semaphores.at[1]).wait()


def left(same_bytes, semaphores):
    pltpu.make_async_copy(same_bytes, same_bytes, semaphores.at[0]).wait()


def sibling():
    slab = lax.axis_index("slab")
    return slab + 1 - 2 * lax.rem(slab, 2), lax.axis_index("sub")


def plane_place():
    return lax.rem(lax.axis_index("slab") // 2, 4) * 4 + lax.axis_index("sub")


def plane_partner(step):
    slab, sub = lax.axis_index("slab"), lax.axis_index("sub")
    y, x = lax.rem(slab // 2 + step[0], 4), lax.rem(sub + step[1], 4)
    return (slab // 8 * 8 + y * 2 + lax.rem(slab, 2), x), y * 4 + x


def column_partner(step):
    slab = lax.axis_index("slab")
    z = lax.rem(slab // 8 + step + DEEP, DEEP)
    return (z * 8 + lax.rem(slab, 8), lax.axis_index("sub")), z


def block_partner(step):
    (slab, sub), _ = plane_partner(step[1:])
    z = lax.rem(slab // 8 + step[0] + DEEP, DEEP)
    return z * 8 + lax.rem(slab, 8), sub


def chunk(ref, place):
    row = pl.multiple_of(place // 4 * 8, 8)
    lane = pl.multiple_of(lax.rem(place, 4) * CHUNK, CHUNK)
    return ref.at[pl.ds(row, 8), pl.ds(lane, CHUNK)]


def tile(ref, place, piece):
    row = pl.multiple_of(place // 4 * 8, 8)
    lane = pl.multiple_of(lax.rem(place, 4) * CHUNK + piece * 128, 128)
    return ref.at[pl.ds(row, 8), pl.ds(lane, 128)]


def half(ref, core):
    return ref.at[pl.ds(pl.multiple_of(core * HALF, HALF), HALF)]


def greet():
    semaphore = pltpu.get_barrier_semaphore()

    def signal(device):
        pl.semaphore_signal(semaphore, inc=1, device_id=device, device_id_type=MESH)

    for direction in DIRECTIONS:
        signal(neighbour(direction))
    signal(sibling())
    for step in ((1, 0), (3, 0)):
        signal(plane_partner(step)[0])
    for step in (1, -1):
        signal(column_partner(step)[0])
    return lambda: pl.semaphore_wait(semaphore, len(DIRECTIONS) + 1 + 2 + 2)


def tell_plane(plane_round_sem, index):
    for step in PLANE_ROUNDS[index]:
        pl.semaphore_signal(
            plane_round_sem.at[index],
            inc=1,
            device_id=plane_partner(step)[0],
            device_id_type=MESH,
        )


def hear_plane(plane_round_sem, index):
    pl.semaphore_wait(plane_round_sem.at[index], len(PLANE_ROUNDS[index]))


def tell(round_sem, index):
    for step in (2**index, -(2**index)):
        pl.semaphore_signal(
            round_sem.at[index],
            inc=1,
            device_id=column_partner(step)[0],
            device_id_type=MESH,
        )


def hear(round_sem, index):
    pl.semaphore_wait(round_sem.at[index], 2)


def kernel(
    features_hbm,
    cotangent_hbm,
    weight_hbm,
    occ_hbm,
    out_ref,
    grad_ref,
    result_ref,
    features_ref,
    cotangent_ref,
    weight_ref,
    occ_ref,
    mask_ref,
    narrow_ref,
    padded_in,
    padded_grad,
    edge_in,
    edge_grad,
    stage_ref,
    shifted_in,
    shifted_grad,
    turned_ref,
    edge_turned_ref,
    forward_ref,
    backward_ref,
    product_ref,
    share_ref,
    face_send,
    face_recv,
    edge_send,
    edge_recv,
    corner_send,
    corner_recv,
    core_recv,
    half_ref,
    plane_recv,
    pieces_ref,
    column_recv,
    gather_bytes,
    full_ref,
    load_sem,
    halo_send_sem,
    halo_recv_sem,
    core_sem,
    plane_sem,
    column_sem,
    gather_sem,
    round_sem,
    plane_round_sem,
):
    loads = [
        pltpu.make_async_copy(features_hbm, features_ref, load_sem.at[0]),
        pltpu.make_async_copy(cotangent_hbm, cotangent_ref, load_sem.at[1]),
        pltpu.make_async_copy(weight_hbm, weight_ref, load_sem.at[2]),
    ]
    flags = pltpu.make_async_copy(occ_hbm, occ_ref, load_sem.at[3])
    slab = lax.axis_index("slab")
    z, core, place = slab // 8, lax.rem(slab, 2), plane_place()
    own = lax.rem(z, PIECES)
    buffers = (face_send, face_recv, edge_send, edge_recv, corner_send, corner_recv)
    halos = halo_copies(buffers, halo_send_sem, halo_recv_sem)
    lanes = (0, 512, 1152, WIDE)
    to_sibling = [
        pltpu.make_async_remote_copy(
            src_ref=half(share_ref, 1 - core).at[:, lanes[a] : lanes[a + 1]],
            dst_ref=core_recv.at[:, lanes[a] : lanes[a + 1]],
            send_sem=core_sem.at[0],
            recv_sem=core_sem.at[1],
            device_id=sibling(),
            device_id_type=MESH,
        )
        for a in range(3)
    ]
    mine = tile(half(full_ref, core), place, own)
    to_plane, to_all = [], []
    for index, step in enumerate(PLANE_STEPS):
        device, other = plane_partner(step)
        to_plane.append(
            pltpu.make_async_remote_copy(
                src_ref=chunk(half_ref, other),
                dst_ref=plane_recv.at[index],
                send_sem=plane_sem.at[0],
                recv_sem=plane_sem.at[1],
                device_id=device,
                device_id_type=MESH,
            )
        )
    for step in NEAR_STEPS:
        to_all.append(
            pltpu.make_async_remote_copy(
                src_ref=mine,
                dst_ref=mine,
                send_sem=gather_sem.at[0],
                recv_sem=gather_sem.at[1],
                device_id=block_partner(step),
                device_id_type=MESH,
            )
        )
    to_column = []
    for step in COLUMN_STEPS:
        device, other = column_partner(step)
        to_column.append(
            pltpu.make_async_remote_copy(
                src_ref=pieces_ref.at[lax.rem(other, PIECES)],
                dst_ref=column_recv.at[z],
                send_sem=column_sem.at[0],
                recv_sem=column_sem.at[1],
                device_id=device,
                device_id_type=MESH,
            )
        )
    column_bytes = column_recv.at[pl.ds(0, DEEP - 1)]

    back_to_sibling = pltpu.make_async_remote_copy(
        src_ref=half(full_ref, core),
        dst_ref=half(full_ref, core),
        send_sem=core_sem.at[2],
        recv_sem=core_sem.at[3],
        device_id=sibling(),
        device_id_type=MESH,
    )

    flags.start()
    for load in loads:
        load.start()
    everyone_here = greet()
    clear_sides(stage_ref, turned_ref, share_ref)
    flags.wait()
    build_masks(occ_ref, mask_ref, narrow_ref)
    for load in loads:
        load.wait()
    cut_faces((features_ref, cotangent_ref), mask_ref, (edge_in, edge_grad), buffers)
    everyone_here()
    for copy in halos:
        copy.start()
    tell(round_sem, 0)
    tell_plane(plane_round_sem, 0)

    raw_refs = (features_ref, cotangent_ref)
    middle = ROWS // 2
    prepare_both(*raw_refs, narrow_ref, shifted_in, turned_ref, range(middle + 1))
    prepare_both(*raw_refs, narrow_ref, shifted_in, turned_ref, range(middle + 1, ROWS))
    inner_gradient(turned_ref, shifted_in, product_ref, 0, middle)
    for side in range(2):
        edge_turned_ref[side] = pairs(edge_grad[side]).T.astype(jnp.bfloat16)
    inner_gradient(turned_ref, shifted_in, product_ref, middle, ROWS)

    hear(round_sem, 0)
    tell(round_sem, 1)
    hear_plane(plane_round_sem, 0)
    tell_plane(plane_round_sem, 1)
    for copy in halos:
        copy.wait()
    place_layers(0, buffers, padded_in)
    for layer in (0, ROWS + 1):
        shift_layer(padded_in, shifted_in, layer, (0, 1, 2))
    stage_edges(0, buffers, stage_ref)
    outer_gradient(
        turned_ref,
        shifted_in,
        edge_turned_ref,
        stage_ref,
        product_ref,
        share_ref,
        lambda a: to_sibling[a].start(),
    )

    build_weights(weight_ref, forward_ref, backward_ref)
    pad_rows(shifted_in, padded_in)
    pltpu.make_async_copy(core_recv, core_recv, core_sem.at[1]).wait()
    hear(round_sem, 1)
    tell(round_sem, 2)
    half_ref[...] = half(share_ref, core)[...] + core_recv[...]
    hear_plane(plane_round_sem, 1)
    start(to_plane)

    place_rows(stage_ref, padded_in)
    shift_rows(padded_in, shifted_in)
    convolve(shifted_in, forward_ref, True, mask_ref, out_ref, 0, 3)
    arrived(plane_recv, plane_sem)
    total = chunk(half_ref, place)[...]
    for index in range(PLANE - 1):
        total = total + plane_recv[index]
    for piece in range(PIECES):
        pieces_ref[piece] = total[:, 128 * piece : 128 * piece + 128]
    hear(round_sem, 2)
    start(to_column)

    convolve(shifted_in, forward_ref, True, mask_ref, out_ref, 3, 4)
    prepare(cotangent_ref, narrow_ref, shifted_grad)
    pad_rows(shifted_grad, padded_grad)
    place_layers(1, buffers, padded_grad)
    stage_edges(1, buffers, stage_ref)
    place_rows(stage_ref, padded_grad)
    shift_rows(padded_grad, shifted_grad)
    for layer in (0, ROWS + 1):
        shift_layer(padded_grad, shifted_grad, layer, (0, 1, 2))
    convolve(shifted_grad, backward_ref, False, mask_ref, grad_ref, 0, 2)
    arrived(column_bytes, column_sem)
    column_recv[z] = pieces_ref[own]
    piece = column_recv[0]
    for index in range(1, DEEP):
        piece = piece + column_recv[index]
    mine[...] = piece
    start(to_all)

    convolve(shifted_grad, backward_ref, False, mask_ref, grad_ref, 2, 4)
    arrived(gather_bytes, gather_sem)
    back_to_sibling.start()
    left(core_recv, core_sem)
    left(plane_recv, plane_sem)
    left(column_bytes, column_sem)
    left(gather_bytes, gather_sem)
    back_to_sibling.wait()
    cells = lax.axis_size("slab") * lax.axis_size("sub") * ROWS * ROWS * BRICK
    result_ref[...] = full_ref[:, : TAPS * C] * cells ** (-0.5)


def scratch():
    bf16, f32, dma = jnp.bfloat16, jnp.float32, pltpu.SemaphoreType.DMA
    return [
        pltpu.VMEM((ROWS, ROWS, XC), bf16),
        pltpu.VMEM((ROWS, ROWS, XC), bf16),
        pltpu.VMEM((C, TAPS * C), bf16),
        pltpu.SMEM((ROWS // BRICK, ROWS // BRICK), jnp.int32),
        pltpu.VMEM((ROWS // BRICK, ROWS, XC), f32),
        pltpu.VMEM((ROWS // BRICK, ROWS, XC), bf16),
        pltpu.VMEM((ROWS + 2, 48, PADX), f32),
        pltpu.VMEM((ROWS + 2, 48, PADX), f32),
        pltpu.VMEM((2, ROWS, XC), f32),
        pltpu.VMEM((2, ROWS, XC), f32),
        pltpu.VMEM((2, 48, PADX), f32),
        pltpu.VMEM((3, (ROWS + 2) * ROWS, PADX), bf16),
        pltpu.VMEM((3, (ROWS + 2) * ROWS, PADX), bf16),
        pltpu.VMEM((3, 128, 128 * (ROWS + 2)), bf16),
        pltpu.VMEM((2, 128, 128), bf16),
        pltpu.VMEM((256, 9 * WINDOW), bf16),
        pltpu.VMEM((9 * WINDOW, 256), bf16),
        pltpu.VMEM((3, 384, 256), f32),
        pltpu.VMEM((C, WIDE), f32),
        pltpu.VMEM((2, 2, ROWS, XC), bf16),
        pltpu.VMEM((2, 2, ROWS, XC), bf16),
        pltpu.VMEM((2, 2, ROWS, XC), bf16),
        pltpu.VMEM((2, 2, ROWS, XC), bf16),
        pltpu.VMEM((4, 8, XC), f32),
        pltpu.VMEM((4, 8, XC), f32),
        pltpu.VMEM((HALF, WIDE), f32),
        pltpu.VMEM((HALF, WIDE), f32),
        pltpu.VMEM((PLANE - 1, 8, CHUNK), f32),
        pltpu.VMEM((PIECES, 8, 128), f32),
        pltpu.VMEM((DEEP, 8, 128), f32),
        pltpu.VMEM((len(NEAR_STEPS), 8, 128), f32),
        pltpu.VMEM((C, WIDE), f32),
        dma((4,)),
        dma((8,)),
        dma((8,)),
        dma((4,)),
        dma((2,)),
        dma((2,)),
        dma((2,)),
        pltpu.SemaphoreType.REGULAR((3,)),
        pltpu.SemaphoreType.REGULAR((2,)),
    ]


def deliver_kernel(*refs):
    sources, targets, semaphores = refs[:3], refs[3:6], refs[6]
    copies = [
        pltpu.make_async_copy(source, target, semaphores.at[index])
        for index, (source, target) in enumerate(zip(sources, targets))
    ]
    for copy in copies:
        copy.start()
    for copy in copies:
        copy.wait()


def deliver(*arrays):
    return pl.pallas_call(
        deliver_kernel,
        out_shape=[jax.ShapeDtypeStruct(a.shape, a.dtype) for a in arrays],
        in_specs=[pl.BlockSpec(memory_space=pltpu.VMEM)] * 3,
        out_specs=[pl.BlockSpec(memory_space=pltpu.HBM)] * 3,
        scratch_shapes=[pltpu.SemaphoreType.DMA((3,))],
        compiler_params=pltpu.CompilerParams(vmem_limit_bytes=8 * 2**20),
        cost_estimate=pl.CostEstimate(
            flops=0, bytes_accessed=5 * 2**20, transcendentals=0
        ),
        name="deliver",
    )(*arrays)


def per_device(features, cotangent, weight, occupancy):
    hbm = pl.BlockSpec(memory_space=pltpu.HBM)
    out, grad, total = pl.pallas_call(
        kernel,
        out_shape=[
            pltpu.VMEM(features.shape, jnp.bfloat16),
            pltpu.VMEM(features.shape, jnp.bfloat16),
            pltpu.VMEM((C, TAPS * C), jnp.float32),
        ],
        in_specs=[hbm] * 4,
        out_specs=[pl.BlockSpec(memory_space=pltpu.VMEM)] * 3,
        scratch_shapes=scratch(),
        compiler_params=pltpu.CompilerParams(
            collective_id=0, has_side_effects=True, vmem_limit_bytes=55 * 2**20
        ),
        cost_estimate=pl.CostEstimate(
            flops=11 * 10**9, bytes_accessed=5 * 2**20, transcendentals=0
        ),
        name="convolutions",
    )(features, cotangent, weight, occupancy)
    return deliver(out, grad, total)


def solution(mesh):
    placed = (P("slab", "sub", None), P("slab", "sub", None), P(), P("slab", "sub"))
    return jax.shard_map(
        per_device,
        mesh=mesh,
        in_specs=placed,
        out_specs=(P("slab", "sub", None), P("slab", "sub", None), P()),
        check_vma=False,
    )
```

```python
import jax
import jax.numpy as jnp
from jax import lax
from jax.experimental import pallas as pl
from jax.experimental.pallas import tpu as pltpu
from jax.sharding import PartitionSpec as P

C = 64
BRICK = 8
ROWS = 32
XC = 512
PADX = XC + 2 * C
WINDOW = 384
TAPS = 27
MESH = pl.DeviceIdType.MESH
DEEP = 16
PLANE = 16
PIECES = 4
CHUNK = 512
WIDE = 4 * CHUNK
PLANE_STEPS = sorted(
    [(dy, dx) for dy in range(4) for dx in range(4) if dy or dx],
    key=lambda step: -min(step[0], 4 - step[0]) - min(step[1], 4 - step[1]),
)
PLANE_ROUNDS = (((0, 1), (0, 3), (1, 0), (3, 0)), ((1, 1), (1, 3), (3, 1), (3, 3)))
COLUMN_STEPS = sorted(range(1, DEEP), key=lambda step: -min(step, DEEP - step))
NEAR_STEPS = sorted(
    [
        (dz, dy, dx)
        for dz in (-2, -1, 0, 1)
        for dy in range(4)
        for dx in range(4)
        if dz or dy or dx
    ],
    key=lambda step: -abs(step[0]) - min(step[1], 4 - step[1]) - min(step[2], 4 - step[2]),
)
HALF = C // 2

FACES_Z = ((1, 0), (-1, 0))
FACES_Y = ((0, 1), (0, -1))
CORNERS = ((1, 1), (1, -1), (-1, 1), (-1, -1))
DIRECTIONS = FACES_Z + FACES_Y + CORNERS


def widen(rows):
    side = jnp.zeros(rows.shape[:-1] + (C,), rows.dtype)
    return jnp.concatenate([side, rows, side], axis=-1)


def pairs(rows):
    return jnp.concatenate([rows[:, 128 * p : 128 * p + 128] for p in range(4)], axis=0)


def pair_windows(rows):
    return jnp.concatenate([rows[:, 128 * p : 128 * p + 256] for p in range(4)], axis=0)


def build_masks(occ_ref, mask_ref, narrow_ref):
    row = lax.broadcasted_iota(jnp.int32, (ROWS, XC), 0) // BRICK
    for brick_z in range(ROWS // BRICK):
        mask = jnp.zeros((ROWS, XC), jnp.float32)
        for brick_y in range(ROWS // BRICK):
            flag = occ_ref[brick_z, brick_y].astype(jnp.float32)
            mask = jnp.where(row == brick_y, flag, mask)
        mask_ref[brick_z] = mask
        narrow_ref[brick_z] = mask.astype(jnp.bfloat16)


def build_weights(w_ref, forward_ref, backward_ref):
    for ab in range(9):
        taps = w_ref[:, 192 * ab : 192 * ab + 192]
        for x in range(4):
            parts = [taps]
            if x > 0:
                parts = [jnp.zeros((C, C * x), taps.dtype)] + parts
            if x < 3:
                parts = parts + [jnp.zeros((C, C * (3 - x)), taps.dtype)]
            forward_ref[C * x : C * x + C, WINDOW * ab : WINDOW * ab + WINDOW] = (
                jnp.concatenate(parts, axis=1)
            )
        mirrored = 8 - ab
        for x in range(6):
            low = C * (x - 2)
            first, last = max(0, -low), min(192, 256 - low)
            parts = [taps[:, first:last]]
            if low > 0:
                parts = [jnp.zeros((C, low), taps.dtype)] + parts
            end = low + last
            if end < 256:
                parts = parts + [jnp.zeros((C, 256 - end), taps.dtype)]
            start = WINDOW * mirrored + C * x
            backward_ref[start : start + C, :] = jnp.concatenate(parts, axis=1)


def clear_sides(stage_ref, turned_ref, share_ref):
    for side in range(2):
        stage_ref[side, 0:8, :] = jnp.zeros((8, PADX), jnp.float32)
        stage_ref[side, 40:48, :] = jnp.zeros((8, PADX), jnp.float32)
    for b in range(3):
        turned_ref[b, :, :128] = jnp.zeros((128, 128), turned_ref.dtype)
        turned_ref[b, :, 128 * (ROWS + 1) :] = jnp.zeros((128, 128), turned_ref.dtype)
    share_ref[:, TAPS * C :] = jnp.zeros((C, WIDE - TAPS * C), jnp.float32)


def cut_faces(raw_refs, mask_ref, edge_refs, buffers):
    face_send, _, edge_send, _, corner_send, _ = buffers

    def layer(z, _):
        mask = mask_ref[z // BRICK]
        for tensor in range(2):
            for side, tile in enumerate((0, ROWS - 16)):
                rows = raw_refs[tensor][z, tile : tile + 16, :].astype(jnp.float32)
                row = 0 if side == 0 else 15
                edge_refs[tensor][side, pl.ds(z, 1), :] = (
                    rows[row : row + 1] * mask[tile + row : tile + row + 1]
                )
        return 0

    lax.fori_loop(0, ROWS, layer, 0, unroll=4)
    for side, z in enumerate((ROWS - 1, 0)):
        for tensor in range(2):
            face = raw_refs[tensor][z].astype(jnp.float32) * mask_ref[z // BRICK]
            face_send[side, tensor] = face.astype(jnp.bfloat16)
            edge_send[side, tensor] = edge_refs[tensor][1 - side].astype(jnp.bfloat16)
    for index, (dz, dy) in enumerate(CORNERS):
        z = ROWS - 1 if dz > 0 else 0
        y = 1 if dy > 0 else 0
        corner_send[index] = jnp.concatenate(
            [edge_refs[0][y, z : z + 1, :], edge_refs[1][y, z : z + 1, :]]
            + [jnp.zeros((6, XC), jnp.float32)],
            axis=0,
        )


def prepare(raw_ref, narrow_ref, shifted_ref, unroll=8):
    def layer(z, _):
        rows = pl.ds(pl.multiple_of((z + 1) * ROWS, ROWS), ROWS)
        shifted_ref[1, rows, :] = widen(raw_ref[z] * narrow_ref[z // BRICK])
        return 0

    lax.fori_loop(0, ROWS, layer, 0, unroll=unroll)


def prepare_both(features_ref, cotangent_ref, narrow_ref, shifted_ref, turned_ref, layers):
    edge = jnp.zeros((128, 1), jnp.bfloat16)
    row = lax.broadcasted_iota(jnp.int32, (128, 128), 1) % ROWS
    not_last = (row != ROWS - 1).astype(jnp.float32).astype(jnp.bfloat16)
    not_first = (row != 0).astype(jnp.float32).astype(jnp.bfloat16)
    for z in layers:
        mask = narrow_ref[z // BRICK]
        shifted_ref[1, ROWS * (z + 1) : ROWS * (z + 2), :] = widen(features_ref[z] * mask)
        column = slice(128 * (z + 1), 128 * (z + 2))
        turned = pairs(cotangent_ref[z] * mask).T
        down = jnp.concatenate([turned[:, 1:], edge], axis=1)
        up = jnp.concatenate([edge, turned[:, :127]], axis=1)
        turned_ref[0, :, column] = not_last * down
        turned_ref[1, :, column] = turned
        turned_ref[2, :, column] = not_first * up


def pad_rows(shifted_ref, padded_ref):
    def layer(z, _):
        rows = pl.ds(pl.multiple_of((z + 1) * ROWS, ROWS), ROWS)
        padded_ref[z + 1, 8:40, :] = shifted_ref[1, rows, :].astype(jnp.float32)
        return 0

    lax.fori_loop(0, ROWS, layer, 0, unroll=4)


def shift_layer(padded_ref, shifted_ref, z, shifts):
    rows = pl.ds(pl.multiple_of(z * ROWS, ROWS), ROWS)
    for b in shifts:
        shifted_ref[b, rows, :] = padded_ref[z, 7 + b : 39 + b, :].astype(jnp.bfloat16)


def shift_rows(padded_ref, shifted_ref):
    def layer(z, _):
        shift_layer(padded_ref, shifted_ref, z, (0, 2))
        return 0

    lax.fori_loop(1, ROWS + 1, layer, 0, unroll=8)


def inner_gradient(turned_ref, shifted_ref, product_ref, first, last):
    window = jnp.concatenate(
        [
            shifted_ref[1, ROWS * z : ROWS * z + ROWS, 128 * p : 128 * p + 256]
            for z in range(first + 1, last + 1)
            for p in range(4)
        ],
        axis=0,
    )
    for b in range(3):
        turned = jnp.concatenate(
            [
                turned_ref[b, :, 128 * (first + 2 - a) : 128 * (last + 2 - a)]
                for a in range(3)
            ],
            axis=0,
        )
        product = jnp.dot(turned, window, preferred_element_type=jnp.float32)
        if first > 0:
            product = product_ref[b] + product
        product_ref[b] = product


def outer_gradient(turned_ref, shifted_ref, edge_turned_ref, stage_ref, product_ref, share_ref, done):
    def along_z(z, layer):
        first = ROWS * layer
        window = jnp.concatenate(
            [pair_windows(shifted_ref[b, first : first + ROWS, :]) for b in range(3)],
            axis=1,
        )
        column = turned_ref[1, :, 128 * (z + 1) : 128 * (z + 2)]
        return jnp.dot(column, window, preferred_element_type=jnp.float32)

    def along_y(side):
        window = jnp.concatenate(
            [
                pair_windows(stage_ref[side, 7 + a : 39 + a, :].astype(jnp.bfloat16))
                for a in range(3)
            ],
            axis=1,
        )
        return jnp.dot(edge_turned_ref[side], window, preferred_element_type=jnp.float32)

    low_z, high_z = along_z(0, 0), along_z(ROWS - 1, ROWS + 1)
    edges = {0: along_y(0), 2: along_y(1)}
    for a in range(3):
        for b in range(3):
            term = product_ref[b, 128 * a : 128 * a + 128, :]
            if a == 0:
                term = term + low_z[:, 256 * b : 256 * b + 256]
            if a == 2:
                term = term + high_z[:, 256 * b : 256 * b + 256]
            if b != 1:
                term = term + edges[b][:, 256 * a : 256 * a + 256]
            ab = 3 * a + b
            share_ref[:, 192 * ab : 192 * ab + 192] = (
                term[:C, :192] + term[C:, C : C + 192]
            )
        done(a)


def convolve(shifted_ref, weight_ref, transposed, mask_ref, out_ref, start, stop, layers=BRICK):
    contract = (((1,), (1 if transposed else 0,)), ((), ()))

    def block(step, _):
        first = step * layers
        mask = mask_ref[first // BRICK, :, :256]
        for quad in range(2):
            window = jnp.concatenate(
                [
                    shifted_ref[
                        b,
                        pl.ds(pl.multiple_of((first + a) * ROWS, ROWS), layers * ROWS),
                        256 * quad : 256 * quad + WINDOW,
                    ]
                    for a in range(3)
                    for b in range(3)
                ],
                axis=1,
            )
            total = lax.dot_general(
                window, weight_ref[...], contract, preferred_element_type=jnp.float32
            )
            total = total.reshape(layers, ROWS, 256) * mask[None]
            out_ref[pl.ds(first, layers), :, 256 * quad : 256 * quad + 256] = total.astype(
                jnp.bfloat16
            )
        return 0

    lax.fori_loop(start, stop, block, 0)


def neighbour(direction):
    slabs, subs = lax.axis_size("slab"), lax.axis_size("sub")
    slab = lax.rem(lax.axis_index("slab") + direction[0] + slabs, slabs)
    sub = lax.rem(lax.axis_index("sub") + direction[1] + subs, subs)
    return slab, sub


def within(direction):
    dz, dy = direction
    inside = jnp.int32(1)
    if dz:
        edge = 0 if dz > 0 else lax.axis_size("slab") - 1
        inside = inside * jnp.where(lax.axis_index("slab") == edge, 0, 1)
    if dy:
        edge = 0 if dy > 0 else lax.axis_size("sub") - 1
        inside = inside * jnp.where(lax.axis_index("sub") == edge, 0, 1)
    return inside.astype(jnp.float32)


def halo_copies(buffers, send_sem, recv_sem):
    face_send, face_recv, edge_send, edge_recv, corner_send, corner_recv = buffers
    pieces = [
        (direction, corner_send.at[index], corner_recv.at[index])
        for index, direction in enumerate(CORNERS)
    ]
    for tensor in range(2):
        for directions, source, target in (
            (FACES_Z, face_send, face_recv),
            (FACES_Y, edge_send, edge_recv),
        ):
            for index, direction in enumerate(directions):
                pieces.append(
                    (direction, source.at[index, tensor], target.at[index, tensor])
                )
    return [
        pltpu.make_async_remote_copy(
            src_ref=source,
            dst_ref=target,
            send_sem=send_sem.at[index],
            recv_sem=recv_sem.at[index],
            device_id=neighbour(direction),
            device_id_type=MESH,
        )
        for index, (direction, source, target) in enumerate(pieces)
    ]


def place_layers(tensor, buffers, padded_ref):
    _, face_recv, _, _, _, corner_recv = buffers
    for index, direction in enumerate(FACES_Z):
        layer = 0 if index == 0 else ROWS + 1
        face = face_recv[index, tensor].astype(jnp.float32) * within(direction)
        padded_ref[layer, 8:40, :] = widen(face)
    for index, direction in enumerate(CORNERS):
        layer = 0 if direction[0] > 0 else ROWS + 1
        row = 7 if direction[1] > 0 else 40
        corner = corner_recv[index, tensor : tensor + 1, :] * within(direction)
        padded_ref[layer, row : row + 1, :] = widen(corner)


def stage_edges(tensor, buffers, stage_ref):
    _, _, _, edge_recv, _, _ = buffers
    for index, direction in enumerate(FACES_Y):
        edge = edge_recv[index, tensor].astype(jnp.float32) * within(direction)
        stage_ref[index, 8:40, :] = widen(edge)


def place_rows(stage_ref, padded_ref):
    def layer(z, _):
        for side, row in enumerate((7, 40)):
            padded_ref[z + 1, row : row + 1, :] = stage_ref[side, pl.ds(8 + z, 1), :]
        return 0

    lax.fori_loop(0, ROWS, layer, 0)


def start(copies):
    for copy in copies:
        copy.start()


def arrived(same_bytes, semaphores):
    pltpu.make_async_copy(same_bytes, same_bytes, semaphores.at[1]).wait()


def left(same_bytes, semaphores):
    pltpu.make_async_copy(same_bytes, same_bytes, semaphores.at[0]).wait()


def sibling():
    slab = lax.axis_index("slab")
    return slab + 1 - 2 * lax.rem(slab, 2), lax.axis_index("sub")


def plane_place():
    return lax.rem(lax.axis_index("slab") // 2, 4) * 4 + lax.axis_index("sub")


def plane_partner(step):
    slab, sub = lax.axis_index("slab"), lax.axis_index("sub")
    y, x = lax.rem(slab // 2 + step[0], 4), lax.rem(sub + step[1], 4)
    return (slab // 8 * 8 + y * 2 + lax.rem(slab, 2), x), y * 4 + x


def column_partner(step):
    slab = lax.axis_index("slab")
    z = lax.rem(slab // 8 + step + DEEP, DEEP)
    return (z * 8 + lax.rem(slab, 8), lax.axis_index("sub")), z


def block_partner(step):
    (slab, sub), _ = plane_partner(step[1:])
    z = lax.rem(slab // 8 + step[0] + DEEP, DEEP)
    return z * 8 + lax.rem(slab, 8), sub


def chunk(ref, place):
    row = pl.multiple_of(place // 4 * 8, 8)
    lane = pl.multiple_of(lax.rem(place, 4) * CHUNK, CHUNK)
    return ref.at[pl.ds(row, 8), pl.ds(lane, CHUNK)]


def tile(ref, place, piece):
    row = pl.multiple_of(place // 4 * 8, 8)
    lane = pl.multiple_of(lax.rem(place, 4) * CHUNK + piece * 128, 128)
    return ref.at[pl.ds(row, 8), pl.ds(lane, 128)]


def half(ref, core):
    return ref.at[pl.ds(pl.multiple_of(core * HALF, HALF), HALF)]


def greet():
    semaphore = pltpu.get_barrier_semaphore()

    def signal(device):
        pl.semaphore_signal(semaphore, inc=1, device_id=device, device_id_type=MESH)

    for direction in DIRECTIONS:
        signal(neighbour(direction))
    signal(sibling())
    for step in ((1, 0), (3, 0)):
        signal(plane_partner(step)[0])
    for step in (1, -1):
        signal(column_partner(step)[0])
    return lambda: pl.semaphore_wait(semaphore, len(DIRECTIONS) + 1 + 2 + 2)


def tell_plane(plane_round_sem, index):
    for step in PLANE_ROUNDS[index]:
        pl.semaphore_signal(
            plane_round_sem.at[index],
            inc=1,
            device_id=plane_partner(step)[0],
            device_id_type=MESH,
        )


def hear_plane(plane_round_sem, index):
    pl.semaphore_wait(plane_round_sem.at[index], len(PLANE_ROUNDS[index]))


def tell(round_sem, index):
    for step in (2**index, -(2**index)):
        pl.semaphore_signal(
            round_sem.at[index],
            inc=1,
            device_id=column_partner(step)[0],
            device_id_type=MESH,
        )


def hear(round_sem, index):
    pl.semaphore_wait(round_sem.at[index], 2)


def kernel(
    features_hbm,
    cotangent_hbm,
    weight_hbm,
    occ_hbm,
    out_ref,
    grad_ref,
    result_ref,
    features_ref,
    cotangent_ref,
    weight_ref,
    occ_ref,
    mask_ref,
    narrow_ref,
    padded_in,
    padded_grad,
    edge_in,
    edge_grad,
    stage_ref,
    shifted_in,
    shifted_grad,
    turned_ref,
    edge_turned_ref,
    forward_ref,
    backward_ref,
    product_ref,
    share_ref,
    face_send,
    face_recv,
    edge_send,
    edge_recv,
    corner_send,
    corner_recv,
    core_recv,
    half_ref,
    plane_recv,
    pieces_ref,
    column_recv,
    gather_bytes,
    full_ref,
    load_sem,
    halo_send_sem,
    halo_recv_sem,
    core_sem,
    plane_sem,
    column_sem,
    gather_sem,
    round_sem,
    plane_round_sem,
):
    loads = [
        pltpu.make_async_copy(features_hbm, features_ref, load_sem.at[0]),
        pltpu.make_async_copy(cotangent_hbm, cotangent_ref, load_sem.at[1]),
        pltpu.make_async_copy(weight_hbm, weight_ref, load_sem.at[2]),
    ]
    flags = pltpu.make_async_copy(occ_hbm, occ_ref, load_sem.at[3])
    slab = lax.axis_index("slab")
    z, core, place = slab // 8, lax.rem(slab, 2), plane_place()
    own = lax.rem(z, PIECES)
    buffers = (face_send, face_recv, edge_send, edge_recv, corner_send, corner_recv)
    halos = halo_copies(buffers, halo_send_sem, halo_recv_sem)
    lanes = (0, 512, 1152, WIDE)
    to_sibling = [
        pltpu.make_async_remote_copy(
            src_ref=half(share_ref, 1 - core).at[:, lanes[a] : lanes[a + 1]],
            dst_ref=core_recv.at[:, lanes[a] : lanes[a + 1]],
            send_sem=core_sem.at[0],
            recv_sem=core_sem.at[1],
            device_id=sibling(),
            device_id_type=MESH,
        )
        for a in range(3)
    ]
    mine = tile(half(full_ref, core), place, own)
    to_plane, to_all = [], []
    for index, step in enumerate(PLANE_STEPS):
        device, other = plane_partner(step)
        to_plane.append(
            pltpu.make_async_remote_copy(
                src_ref=chunk(half_ref, other),
                dst_ref=plane_recv.at[index],
                send_sem=plane_sem.at[0],
                recv_sem=plane_sem.at[1],
                device_id=device,
                device_id_type=MESH,
            )
        )
    for step in NEAR_STEPS:
        to_all.append(
            pltpu.make_async_remote_copy(
                src_ref=mine,
                dst_ref=mine,
                send_sem=gather_sem.at[0],
                recv_sem=gather_sem.at[1],
                device_id=block_partner(step),
                device_id_type=MESH,
            )
        )
    to_column = []
    for step in COLUMN_STEPS:
        device, other = column_partner(step)
        to_column.append(
            pltpu.make_async_remote_copy(
                src_ref=pieces_ref.at[lax.rem(other, PIECES)],
                dst_ref=column_recv.at[z],
                send_sem=column_sem.at[0],
                recv_sem=column_sem.at[1],
                device_id=device,
                device_id_type=MESH,
            )
        )
    column_bytes = column_recv.at[pl.ds(0, DEEP - 1)]

    back_to_sibling = pltpu.make_async_remote_copy(
        src_ref=half(full_ref, core),
        dst_ref=half(full_ref, core),
        send_sem=core_sem.at[2],
        recv_sem=core_sem.at[3],
        device_id=sibling(),
        device_id_type=MESH,
    )

    flags.start()
    for load in loads:
        load.start()
    everyone_here = greet()
    clear_sides(stage_ref, turned_ref, share_ref)
    flags.wait()
    build_masks(occ_ref, mask_ref, narrow_ref)
    for load in loads:
        load.wait()
    cut_faces((features_ref, cotangent_ref), mask_ref, (edge_in, edge_grad), buffers)
    everyone_here()
    for copy in halos:
        copy.start()
    tell(round_sem, 0)
    tell_plane(plane_round_sem, 0)

    raw_refs = (features_ref, cotangent_ref)
    middle = ROWS // 2
    prepare_both(*raw_refs, narrow_ref, shifted_in, turned_ref, range(middle + 1))
    prepare_both(*raw_refs, narrow_ref, shifted_in, turned_ref, range(middle + 1, ROWS))
    inner_gradient(turned_ref, shifted_in, product_ref, 0, middle)
    for side in range(2):
        edge_turned_ref[side] = pairs(edge_grad[side]).T.astype(jnp.bfloat16)
    inner_gradient(turned_ref, shifted_in, product_ref, middle, ROWS)

    hear(round_sem, 0)
    tell(round_sem, 1)
    hear_plane(plane_round_sem, 0)
    tell_plane(plane_round_sem, 1)
    for copy in halos[:8]:
        copy.wait_recv()
    place_layers(0, buffers, padded_in)
    for layer in (0, ROWS + 1):
        shift_layer(padded_in, shifted_in, layer, (0, 1, 2))
    stage_edges(0, buffers, stage_ref)
    outer_gradient(
        turned_ref,
        shifted_in,
        edge_turned_ref,
        stage_ref,
        product_ref,
        share_ref,
        lambda a: to_sibling[a].start(),
    )

    build_weights(weight_ref, forward_ref, backward_ref)
    pad_rows(shifted_in, padded_in)
    pltpu.make_async_copy(core_recv, core_recv, core_sem.at[1]).wait()
    hear(round_sem, 1)
    tell(round_sem, 2)
    half_ref[...] = half(share_ref, core)[...] + core_recv[...]
    hear_plane(plane_round_sem, 1)
    start(to_plane)

    place_rows(stage_ref, padded_in)
    shift_rows(padded_in, shifted_in)
    convolve(shifted_in, forward_ref, True, mask_ref, out_ref, 0, 3)
    arrived(plane_recv, plane_sem)
    total = chunk(half_ref, place)[...]
    for index in range(PLANE - 1):
        total = total + plane_recv[index]
    for piece in range(PIECES):
        pieces_ref[piece] = total[:, 128 * piece : 128 * piece + 128]
    hear(round_sem, 2)
    start(to_column)

    convolve(shifted_in, forward_ref, True, mask_ref, out_ref, 3, 4)
    prepare(cotangent_ref, narrow_ref, shifted_grad)
    pad_rows(shifted_grad, padded_grad)
    for copy in halos[8:]:
        copy.wait_recv()
    for copy in halos:
        copy.wait_send()
    place_layers(1, buffers, padded_grad)
    stage_edges(1, buffers, stage_ref)
    place_rows(stage_ref, padded_grad)
    shift_rows(padded_grad, shifted_grad)
    for layer in (0, ROWS + 1):
        shift_layer(padded_grad, shifted_grad, layer, (0, 1, 2))
    convolve(shifted_grad, backward_ref, False, mask_ref, grad_ref, 0, 2)
    arrived(column_bytes, column_sem)
    column_recv[z] = pieces_ref[own]
    piece = column_recv[0]
    for index in range(1, DEEP):
        piece = piece + column_recv[index]
    mine[...] = piece
    start(to_all)

    convolve(shifted_grad, backward_ref, False, mask_ref, grad_ref, 2, 4)
    arrived(gather_bytes, gather_sem)
    back_to_sibling.start()
    left(core_recv, core_sem)
    left(plane_recv, plane_sem)
    left(column_bytes, column_sem)
    left(gather_bytes, gather_sem)
    back_to_sibling.wait()
    cells = lax.axis_size("slab") * lax.axis_size("sub") * ROWS * ROWS * BRICK
    result_ref[...] = full_ref[:, : TAPS * C] * cells ** (-0.5)


def scratch():
    bf16, f32, dma = jnp.bfloat16, jnp.float32, pltpu.SemaphoreType.DMA
    return [
        pltpu.VMEM((ROWS, ROWS, XC), bf16),
        pltpu.VMEM((ROWS, ROWS, XC), bf16),
        pltpu.VMEM((C, TAPS * C), bf16),
        pltpu.SMEM((ROWS // BRICK, ROWS // BRICK), jnp.int32),
        pltpu.VMEM((ROWS // BRICK, ROWS, XC), f32),
        pltpu.VMEM((ROWS // BRICK, ROWS, XC), bf16),
        pltpu.VMEM((ROWS + 2, 48, PADX), f32),
        pltpu.VMEM((ROWS + 2, 48, PADX), f32),
        pltpu.VMEM((2, ROWS, XC), f32),
        pltpu.VMEM((2, ROWS, XC), f32),
        pltpu.VMEM((2, 48, PADX), f32),
        pltpu.VMEM((3, (ROWS + 2) * ROWS, PADX), bf16),
        pltpu.VMEM((3, (ROWS + 2) * ROWS, PADX), bf16),
        pltpu.VMEM((3, 128, 128 * (ROWS + 2)), bf16),
        pltpu.VMEM((2, 128, 128), bf16),
        pltpu.VMEM((256, 9 * WINDOW), bf16),
        pltpu.VMEM((9 * WINDOW, 256), bf16),
        pltpu.VMEM((3, 384, 256), f32),
        pltpu.VMEM((C, WIDE), f32),
        pltpu.VMEM((2, 2, ROWS, XC), bf16),
        pltpu.VMEM((2, 2, ROWS, XC), bf16),
        pltpu.VMEM((2, 2, ROWS, XC), bf16),
        pltpu.VMEM((2, 2, ROWS, XC), bf16),
        pltpu.VMEM((4, 8, XC), f32),
        pltpu.VMEM((4, 8, XC), f32),
        pltpu.VMEM((HALF, WIDE), f32),
        pltpu.VMEM((HALF, WIDE), f32),
        pltpu.VMEM((PLANE - 1, 8, CHUNK), f32),
        pltpu.VMEM((PIECES, 8, 128), f32),
        pltpu.VMEM((DEEP, 8, 128), f32),
        pltpu.VMEM((len(NEAR_STEPS), 8, 128), f32),
        pltpu.VMEM((C, WIDE), f32),
        dma((4,)),
        dma((12,)),
        dma((12,)),
        dma((4,)),
        dma((2,)),
        dma((2,)),
        dma((2,)),
        pltpu.SemaphoreType.REGULAR((3,)),
        pltpu.SemaphoreType.REGULAR((2,)),
    ]


def deliver_kernel(*refs):
    sources, targets, semaphores = refs[:3], refs[3:6], refs[6]
    copies = [
        pltpu.make_async_copy(source, target, semaphores.at[index])
        for index, (source, target) in enumerate(zip(sources, targets))
    ]
    for copy in copies:
        copy.start()
    for copy in copies:
        copy.wait()


def deliver(*arrays):
    return pl.pallas_call(
        deliver_kernel,
        out_shape=[jax.ShapeDtypeStruct(a.shape, a.dtype) for a in arrays],
        in_specs=[pl.BlockSpec(memory_space=pltpu.VMEM)] * 3,
        out_specs=[pl.BlockSpec(memory_space=pltpu.HBM)] * 3,
        scratch_shapes=[pltpu.SemaphoreType.DMA((3,))],
        compiler_params=pltpu.CompilerParams(vmem_limit_bytes=8 * 2**20),
        cost_estimate=pl.CostEstimate(
            flops=0, bytes_accessed=5 * 2**20, transcendentals=0
        ),
        name="deliver",
    )(*arrays)


def per_device(features, cotangent, weight, occupancy):
    hbm = pl.BlockSpec(memory_space=pltpu.HBM)
    out, grad, total = pl.pallas_call(
        kernel,
        out_shape=[
            pltpu.VMEM(features.shape, jnp.bfloat16),
            pltpu.VMEM(features.shape, jnp.bfloat16),
            pltpu.VMEM((C, TAPS * C), jnp.float32),
        ],
        in_specs=[hbm] * 4,
        out_specs=[pl.BlockSpec(memory_space=pltpu.VMEM)] * 3,
        scratch_shapes=scratch(),
        compiler_params=pltpu.CompilerParams(
            collective_id=0, has_side_effects=True, vmem_limit_bytes=55 * 2**20
        ),
        cost_estimate=pl.CostEstimate(
            flops=11 * 10**9, bytes_accessed=5 * 2**20, transcendentals=0
        ),
        name="convolutions",
    )(features, cotangent, weight, occupancy)
    return deliver(out, grad, total)


def solution(mesh):
    placed = (P("slab", "sub", None), P("slab", "sub", None), P(), P("slab", "sub"))
    return jax.shard_map(
        per_device,
        mesh=mesh,
        in_specs=placed,
        out_specs=(P("slab", "sub", None), P("slab", "sub", None), P()),
        check_vma=False,
    )
```

```python
import jax
import jax.numpy as jnp
from jax import lax
from jax.experimental import pallas as pl
from jax.experimental.pallas import tpu as pltpu
from jax.sharding import PartitionSpec as P

C = 64
BRICK = 8
ROWS = 32
XC = 512
PADX = XC + 2 * C
WINDOW = 384
TAPS = 27
MESH = pl.DeviceIdType.MESH
DEEP = 16
PLANE = 16
PIECES = 4
CHUNK = 512
WIDE = 4 * CHUNK
PLANE_STEPS = sorted(
    [(dy, dx) for dy in range(4) for dx in range(4) if dy or dx],
    key=lambda step: -min(step[0], 4 - step[0]) - min(step[1], 4 - step[1]),
)
PLANE_ROUNDS = (((0, 1), (0, 3), (1, 0), (3, 0)), ((1, 1), (1, 3), (3, 1), (3, 3)))
COLUMN_STEPS = sorted(range(1, DEEP), key=lambda step: -min(step, DEEP - step))
NEAR_STEPS = sorted(
    [
        (dz, dy, dx)
        for dz in (-2, -1, 0, 1)
        for dy in range(4)
        for dx in range(4)
        if dz or dy or dx
    ],
    key=lambda step: -abs(step[0]) - min(step[1], 4 - step[1]) - min(step[2], 4 - step[2]),
)
HALF = C // 2

FACES_Z = ((1, 0), (-1, 0))
FACES_Y = ((0, 1), (0, -1))
CORNERS = ((1, 1), (1, -1), (-1, 1), (-1, -1))
DIRECTIONS = FACES_Z + FACES_Y + CORNERS


def widen(rows):
    side = jnp.zeros(rows.shape[:-1] + (C,), rows.dtype)
    return jnp.concatenate([side, rows, side], axis=-1)


def pairs(rows):
    return jnp.concatenate([rows[:, 128 * p : 128 * p + 128] for p in range(4)], axis=0)


def pair_windows(rows):
    return jnp.concatenate([rows[:, 128 * p : 128 * p + 256] for p in range(4)], axis=0)


def build_masks(occ_ref, mask_ref, narrow_ref):
    row = lax.broadcasted_iota(jnp.int32, (ROWS, XC), 0) // BRICK
    for brick_z in range(ROWS // BRICK):
        mask = jnp.zeros((ROWS, XC), jnp.float32)
        for brick_y in range(ROWS // BRICK):
            flag = occ_ref[brick_z, brick_y].astype(jnp.float32)
            mask = jnp.where(row == brick_y, flag, mask)
        mask_ref[brick_z] = mask
        narrow_ref[brick_z] = mask.astype(jnp.bfloat16)


def build_weights(w_ref, forward_ref, backward_ref):
    for ab in range(9):
        taps = w_ref[:, 192 * ab : 192 * ab + 192]
        for x in range(4):
            parts = [taps]
            if x > 0:
                parts = [jnp.zeros((C, C * x), taps.dtype)] + parts
            if x < 3:
                parts = parts + [jnp.zeros((C, C * (3 - x)), taps.dtype)]
            forward_ref[C * x : C * x + C, WINDOW * ab : WINDOW * ab + WINDOW] = (
                jnp.concatenate(parts, axis=1)
            )
        mirrored = 8 - ab
        for x in range(6):
            low = C * (x - 2)
            first, last = max(0, -low), min(192, 256 - low)
            parts = [taps[:, first:last]]
            if low > 0:
                parts = [jnp.zeros((C, low), taps.dtype)] + parts
            end = low + last
            if end < 256:
                parts = parts + [jnp.zeros((C, 256 - end), taps.dtype)]
            start = WINDOW * mirrored + C * x
            backward_ref[start : start + C, :] = jnp.concatenate(parts, axis=1)


def clear_sides(stage_ref, turned_ref, share_ref):
    for side in range(2):
        stage_ref[side, 0:8, :] = jnp.zeros((8, PADX), jnp.float32)
        stage_ref[side, 40:48, :] = jnp.zeros((8, PADX), jnp.float32)
    for b in range(3):
        turned_ref[b, :, :128] = jnp.zeros((128, 128), turned_ref.dtype)
        turned_ref[b, :, 128 * (ROWS + 1) :] = jnp.zeros((128, 128), turned_ref.dtype)
    share_ref[:, TAPS * C :] = jnp.zeros((C, WIDE - TAPS * C), jnp.float32)


def cut_faces(raw_refs, mask_ref, edge_refs, buffers):
    face_send, _, edge_send, _, corner_send, _ = buffers

    def layer(z, _):
        mask = mask_ref[z // BRICK]
        for tensor in range(2):
            for side, tile in enumerate((0, ROWS - 16)):
                rows = raw_refs[tensor][z, tile : tile + 16, :].astype(jnp.float32)
                row = 0 if side == 0 else 15
                edge_refs[tensor][side, pl.ds(z, 1), :] = (
                    rows[row : row + 1] * mask[tile + row : tile + row + 1]
                )
        return 0

    lax.fori_loop(0, ROWS, layer, 0, unroll=4)
    for side, z in enumerate((ROWS - 1, 0)):
        for tensor in range(2):
            face = raw_refs[tensor][z].astype(jnp.float32) * mask_ref[z // BRICK]
            face_send[side, tensor] = face.astype(jnp.bfloat16)
            edge_send[side, tensor] = edge_refs[tensor][1 - side].astype(jnp.bfloat16)
    for index, (dz, dy) in enumerate(CORNERS):
        z = ROWS - 1 if dz > 0 else 0
        y = 1 if dy > 0 else 0
        corner_send[index] = jnp.concatenate(
            [edge_refs[0][y, z : z + 1, :], edge_refs[1][y, z : z + 1, :]]
            + [jnp.zeros((6, XC), jnp.float32)],
            axis=0,
        )


def prepare(raw_ref, narrow_ref, shifted_ref, unroll=8):
    def layer(z, _):
        rows = pl.ds(pl.multiple_of((z + 1) * ROWS, ROWS), ROWS)
        shifted_ref[1, rows, :] = widen(raw_ref[z] * narrow_ref[z // BRICK])
        return 0

    lax.fori_loop(0, ROWS, layer, 0, unroll=unroll)


def prepare_both(features_ref, cotangent_ref, narrow_ref, shifted_ref, turned_ref, layers):
    edge = jnp.zeros((128, 1), jnp.bfloat16)
    row = lax.broadcasted_iota(jnp.int32, (128, 128), 1) % ROWS
    not_last = (row != ROWS - 1).astype(jnp.float32).astype(jnp.bfloat16)
    not_first = (row != 0).astype(jnp.float32).astype(jnp.bfloat16)
    for z in layers:
        mask = narrow_ref[z // BRICK]
        shifted_ref[1, ROWS * (z + 1) : ROWS * (z + 2), :] = widen(features_ref[z] * mask)
        column = slice(128 * (z + 1), 128 * (z + 2))
        turned = pairs(cotangent_ref[z] * mask).T
        down = jnp.concatenate([turned[:, 1:], edge], axis=1)
        up = jnp.concatenate([edge, turned[:, :127]], axis=1)
        turned_ref[0, :, column] = not_last * down
        turned_ref[1, :, column] = turned
        turned_ref[2, :, column] = not_first * up


def pad_rows(shifted_ref, padded_ref):
    def layer(z, _):
        rows = pl.ds(pl.multiple_of((z + 1) * ROWS, ROWS), ROWS)
        padded_ref[z + 1, 8:40, :] = shifted_ref[1, rows, :].astype(jnp.float32)
        return 0

    lax.fori_loop(0, ROWS, layer, 0, unroll=4)


def shift_layer(padded_ref, shifted_ref, z, shifts):
    rows = pl.ds(pl.multiple_of(z * ROWS, ROWS), ROWS)
    for b in shifts:
        shifted_ref[b, rows, :] = padded_ref[z, 7 + b : 39 + b, :].astype(jnp.bfloat16)


def shift_rows(padded_ref, shifted_ref):
    def layer(z, _):
        shift_layer(padded_ref, shifted_ref, z, (0, 2))
        return 0

    lax.fori_loop(1, ROWS + 1, layer, 0, unroll=8)


def inner_gradient(turned_ref, shifted_ref, product_ref, first, last):
    window = jnp.concatenate(
        [
            shifted_ref[1, ROWS * z : ROWS * z + ROWS, 128 * p : 128 * p + 256]
            for z in range(first + 1, last + 1)
            for p in range(4)
        ],
        axis=0,
    )
    for b in range(3):
        turned = jnp.concatenate(
            [
                turned_ref[b, :, 128 * (first + 2 - a) : 128 * (last + 2 - a)]
                for a in range(3)
            ],
            axis=0,
        )
        product = jnp.dot(turned, window, preferred_element_type=jnp.float32)
        if first > 0:
            product = product_ref[b] + product
        product_ref[b] = product


def outer_gradient(turned_ref, shifted_ref, edge_turned_ref, stage_ref, product_ref, share_ref, done):
    def along_z(z, layer):
        first = ROWS * layer
        window = jnp.concatenate(
            [pair_windows(shifted_ref[b, first : first + ROWS, :]) for b in range(3)],
            axis=1,
        )
        column = turned_ref[1, :, 128 * (z + 1) : 128 * (z + 2)]
        return jnp.dot(column, window, preferred_element_type=jnp.float32)

    def along_y(side):
        window = jnp.concatenate(
            [
                pair_windows(stage_ref[side, 7 + a : 39 + a, :].astype(jnp.bfloat16))
                for a in range(3)
            ],
            axis=1,
        )
        return jnp.dot(edge_turned_ref[side], window, preferred_element_type=jnp.float32)

    low_z, high_z = along_z(0, 0), along_z(ROWS - 1, ROWS + 1)
    edges = {0: along_y(0), 2: along_y(1)}
    for a in range(3):
        for b in range(3):
            term = product_ref[b, 128 * a : 128 * a + 128, :]
            if a == 0:
                term = term + low_z[:, 256 * b : 256 * b + 256]
            if a == 2:
                term = term + high_z[:, 256 * b : 256 * b + 256]
            if b != 1:
                term = term + edges[b][:, 256 * a : 256 * a + 256]
            ab = 3 * a + b
            share_ref[:, 192 * ab : 192 * ab + 192] = (
                term[:C, :192] + term[C:, C : C + 192]
            )
        done(a)


def convolve(shifted_ref, weight_ref, transposed, mask_ref, out_ref, start, stop, layers=BRICK):
    contract = (((1,), (1 if transposed else 0,)), ((), ()))

    def block(step, _):
        first = step * layers
        mask = mask_ref[first // BRICK, :, :256]
        for quad in range(2):
            window = jnp.concatenate(
                [
                    shifted_ref[
                        b,
                        pl.ds(pl.multiple_of((first + a) * ROWS, ROWS), layers * ROWS),
                        256 * quad : 256 * quad + WINDOW,
                    ]
                    for a in range(3)
                    for b in range(3)
                ],
                axis=1,
            )
            total = lax.dot_general(
                window, weight_ref[...], contract, preferred_element_type=jnp.float32
            )
            total = total.reshape(layers, ROWS, 256) * mask[None]
            out_ref[pl.ds(first, layers), :, 256 * quad : 256 * quad + 256] = total.astype(
                jnp.bfloat16
            )
        return 0

    lax.fori_loop(start, stop, block, 0)


def neighbour(direction):
    slabs, subs = lax.axis_size("slab"), lax.axis_size("sub")
    slab = lax.rem(lax.axis_index("slab") + direction[0] + slabs, slabs)
    sub = lax.rem(lax.axis_index("sub") + direction[1] + subs, subs)
    return slab, sub


def within(direction):
    dz, dy = direction
    inside = jnp.int32(1)
    if dz:
        edge = 0 if dz > 0 else lax.axis_size("slab") - 1
        inside = inside * jnp.where(lax.axis_index("slab") == edge, 0, 1)
    if dy:
        edge = 0 if dy > 0 else lax.axis_size("sub") - 1
        inside = inside * jnp.where(lax.axis_index("sub") == edge, 0, 1)
    return inside.astype(jnp.float32)


def halo_copies(buffers, send_sem, recv_sem):
    face_send, face_recv, edge_send, edge_recv, corner_send, corner_recv = buffers
    pieces = [
        (direction, corner_send.at[index], corner_recv.at[index])
        for index, direction in enumerate(CORNERS)
    ]
    for tensor in range(2):
        for directions, source, target in (
            (FACES_Z, face_send, face_recv),
            (FACES_Y, edge_send, edge_recv),
        ):
            for index, direction in enumerate(directions):
                pieces.append(
                    (direction, source.at[index, tensor], target.at[index, tensor])
                )
    return [
        pltpu.make_async_remote_copy(
            src_ref=source,
            dst_ref=target,
            send_sem=send_sem.at[index],
            recv_sem=recv_sem.at[index],
            device_id=neighbour(direction),
            device_id_type=MESH,
        )
        for index, (direction, source, target) in enumerate(pieces)
    ]


def place_layers(tensor, buffers, padded_ref):
    _, face_recv, _, _, _, corner_recv = buffers
    for index, direction in enumerate(FACES_Z):
        layer = 0 if index == 0 else ROWS + 1
        face = face_recv[index, tensor].astype(jnp.float32) * within(direction)
        padded_ref[layer, 8:40, :] = widen(face)
    for index, direction in enumerate(CORNERS):
        layer = 0 if direction[0] > 0 else ROWS + 1
        row = 7 if direction[1] > 0 else 40
        corner = corner_recv[index, tensor : tensor + 1, :] * within(direction)
        padded_ref[layer, row : row + 1, :] = widen(corner)


def stage_edges(tensor, buffers, stage_ref):
    _, _, _, edge_recv, _, _ = buffers
    for index, direction in enumerate(FACES_Y):
        edge = edge_recv[index, tensor].astype(jnp.float32) * within(direction)
        stage_ref[index, 8:40, :] = widen(edge)


def place_rows(stage_ref, padded_ref):
    def layer(z, _):
        for side, row in enumerate((7, 40)):
            padded_ref[z + 1, row : row + 1, :] = stage_ref[side, pl.ds(8 + z, 1), :]
        return 0

    lax.fori_loop(0, ROWS, layer, 0)


def start(copies):
    for copy in copies:
        copy.start()


def arrived(same_bytes, semaphores):
    pltpu.make_async_copy(same_bytes, same_bytes, semaphores.at[1]).wait()


def left(same_bytes, semaphores):
    pltpu.make_async_copy(same_bytes, same_bytes, semaphores.at[0]).wait()


def sibling():
    slab = lax.axis_index("slab")
    return slab + 1 - 2 * lax.rem(slab, 2), lax.axis_index("sub")


def plane_place():
    return lax.rem(lax.axis_index("slab") // 2, 4) * 4 + lax.axis_index("sub")


def plane_partner(step):
    slab, sub = lax.axis_index("slab"), lax.axis_index("sub")
    y, x = lax.rem(slab // 2 + step[0], 4), lax.rem(sub + step[1], 4)
    return (slab // 8 * 8 + y * 2 + lax.rem(slab, 2), x), y * 4 + x


def column_partner(step):
    slab = lax.axis_index("slab")
    z = lax.rem(slab // 8 + step + DEEP, DEEP)
    return (z * 8 + lax.rem(slab, 8), lax.axis_index("sub")), z


def block_partner(step):
    (slab, sub), _ = plane_partner(step[1:])
    z = lax.rem(slab // 8 + step[0] + DEEP, DEEP)
    return z * 8 + lax.rem(slab, 8), sub


def chunk(ref, place):
    row = pl.multiple_of(place // 4 * 8, 8)
    lane = pl.multiple_of(lax.rem(place, 4) * CHUNK, CHUNK)
    return ref.at[pl.ds(row, 8), pl.ds(lane, CHUNK)]


def tile(ref, place, piece):
    row = pl.multiple_of(place // 4 * 8, 8)
    lane = pl.multiple_of(lax.rem(place, 4) * CHUNK + piece * 128, 128)
    return ref.at[pl.ds(row, 8), pl.ds(lane, 128)]


def half(ref, core):
    return ref.at[pl.ds(pl.multiple_of(core * HALF, HALF), HALF)]


def greet():
    semaphore = pltpu.get_barrier_semaphore()

    def signal(device):
        pl.semaphore_signal(semaphore, inc=1, device_id=device, device_id_type=MESH)

    for direction in CORNERS + FACES_Z + FACES_Y:
        signal(neighbour(direction))
    signal(sibling())
    for step in ((1, 0), (3, 0)):
        signal(plane_partner(step)[0])
    for step in (1, -1):
        signal(column_partner(step)[0])
    return lambda: pl.semaphore_wait(semaphore, len(DIRECTIONS) + 1 + 2 + 2)


def tell_plane(plane_round_sem, index):
    for step in PLANE_ROUNDS[index]:
        pl.semaphore_signal(
            plane_round_sem.at[index],
            inc=1,
            device_id=plane_partner(step)[0],
            device_id_type=MESH,
        )


def hear_plane(plane_round_sem, index):
    pl.semaphore_wait(plane_round_sem.at[index], len(PLANE_ROUNDS[index]))


def tell(round_sem, index):
    for step in (2**index, -(2**index)):
        pl.semaphore_signal(
            round_sem.at[index],
            inc=1,
            device_id=column_partner(step)[0],
            device_id_type=MESH,
        )


def hear(round_sem, index):
    pl.semaphore_wait(round_sem.at[index], 2)


def kernel(
    features_hbm,
    cotangent_hbm,
    weight_hbm,
    occ_hbm,
    out_ref,
    grad_ref,
    result_ref,
    features_ref,
    cotangent_ref,
    weight_ref,
    occ_ref,
    mask_ref,
    narrow_ref,
    padded_in,
    padded_grad,
    edge_in,
    edge_grad,
    stage_ref,
    shifted_in,
    shifted_grad,
    turned_ref,
    edge_turned_ref,
    forward_ref,
    backward_ref,
    product_ref,
    share_ref,
    face_send,
    face_recv,
    edge_send,
    edge_recv,
    corner_send,
    corner_recv,
    core_recv,
    half_ref,
    plane_recv,
    pieces_ref,
    column_recv,
    gather_bytes,
    full_ref,
    load_sem,
    halo_send_sem,
    halo_recv_sem,
    core_sem,
    plane_sem,
    column_sem,
    gather_sem,
    round_sem,
    plane_round_sem,
):
    loads = [
        pltpu.make_async_copy(features_hbm, features_ref, load_sem.at[0]),
        pltpu.make_async_copy(cotangent_hbm, cotangent_ref, load_sem.at[1]),
    ]
    weight_load = pltpu.make_async_copy(weight_hbm, weight_ref, load_sem.at[2])
    flags = pltpu.make_async_copy(occ_hbm, occ_ref, load_sem.at[3])
    slab = lax.axis_index("slab")
    z, core, place = slab // 8, lax.rem(slab, 2), plane_place()
    own = lax.rem(z, PIECES)
    buffers = (face_send, face_recv, edge_send, edge_recv, corner_send, corner_recv)
    halos = halo_copies(buffers, halo_send_sem, halo_recv_sem)
    lanes = (0, 512, 1152, WIDE)
    to_sibling = [
        pltpu.make_async_remote_copy(
            src_ref=half(share_ref, 1 - core).at[:, lanes[a] : lanes[a + 1]],
            dst_ref=core_recv.at[:, lanes[a] : lanes[a + 1]],
            send_sem=core_sem.at[0],
            recv_sem=core_sem.at[1],
            device_id=sibling(),
            device_id_type=MESH,
        )
        for a in range(3)
    ]
    mine = tile(half(full_ref, core), place, own)
    to_plane, to_all = [], []
    for index, step in enumerate(PLANE_STEPS):
        device, other = plane_partner(step)
        to_plane.append(
            pltpu.make_async_remote_copy(
                src_ref=chunk(half_ref, other),
                dst_ref=plane_recv.at[index],
                send_sem=plane_sem.at[0],
                recv_sem=plane_sem.at[1],
                device_id=device,
                device_id_type=MESH,
            )
        )
    for step in NEAR_STEPS:
        to_all.append(
            pltpu.make_async_remote_copy(
                src_ref=mine,
                dst_ref=mine,
                send_sem=gather_sem.at[0],
                recv_sem=gather_sem.at[1],
                device_id=block_partner(step),
                device_id_type=MESH,
            )
        )
    to_column = []
    for step in COLUMN_STEPS:
        device, other = column_partner(step)
        to_column.append(
            pltpu.make_async_remote_copy(
                src_ref=pieces_ref.at[lax.rem(other, PIECES)],
                dst_ref=column_recv.at[z],
                send_sem=column_sem.at[0],
                recv_sem=column_sem.at[1],
                device_id=device,
                device_id_type=MESH,
            )
        )
    column_bytes = column_recv.at[pl.ds(0, DEEP - 1)]

    back_to_sibling = pltpu.make_async_remote_copy(
        src_ref=half(full_ref, core),
        dst_ref=half(full_ref, core),
        send_sem=core_sem.at[2],
        recv_sem=core_sem.at[3],
        device_id=sibling(),
        device_id_type=MESH,
    )

    flags.start()
    for load in loads:
        load.start()
    everyone_here = greet()
    clear_sides(stage_ref, turned_ref, share_ref)
    flags.wait()
    build_masks(occ_ref, mask_ref, narrow_ref)
    for load in loads:
        load.wait()
    cut_faces((features_ref, cotangent_ref), mask_ref, (edge_in, edge_grad), buffers)
    everyone_here()
    for copy in halos:
        copy.start()
    weight_load.start()
    tell(round_sem, 0)
    tell_plane(plane_round_sem, 0)

    raw_refs = (features_ref, cotangent_ref)
    middle = ROWS // 2
    prepare_both(*raw_refs, narrow_ref, shifted_in, turned_ref, range(middle + 1))
    prepare_both(*raw_refs, narrow_ref, shifted_in, turned_ref, range(middle + 1, ROWS))
    inner_gradient(turned_ref, shifted_in, product_ref, 0, middle)
    for side in range(2):
        edge_turned_ref[side] = pairs(edge_grad[side]).T.astype(jnp.bfloat16)
    inner_gradient(turned_ref, shifted_in, product_ref, middle, ROWS)

    hear(round_sem, 0)
    tell(round_sem, 1)
    hear_plane(plane_round_sem, 0)
    tell_plane(plane_round_sem, 1)
    for copy in halos[:8]:
        copy.wait_recv()
    place_layers(0, buffers, padded_in)
    for layer in (0, ROWS + 1):
        shift_layer(padded_in, shifted_in, layer, (0, 1, 2))
    stage_edges(0, buffers, stage_ref)
    outer_gradient(
        turned_ref,
        shifted_in,
        edge_turned_ref,
        stage_ref,
        product_ref,
        share_ref,
        lambda a: to_sibling[a].start(),
    )

    weight_load.wait()
    build_weights(weight_ref, forward_ref, backward_ref)
    pad_rows(shifted_in, padded_in)
    pltpu.make_async_copy(core_recv, core_recv, core_sem.at[1]).wait()
    hear(round_sem, 1)
    tell(round_sem, 2)
    half_ref[...] = half(share_ref, core)[...] + core_recv[...]
    hear_plane(plane_round_sem, 1)
    start(to_plane)

    place_rows(stage_ref, padded_in)
    shift_rows(padded_in, shifted_in)
    convolve(shifted_in, forward_ref, True, mask_ref, out_ref, 0, 3)
    arrived(plane_recv, plane_sem)
    total = chunk(half_ref, place)[...]
    for index in range(PLANE - 1):
        total = total + plane_recv[index]
    for piece in range(PIECES):
        pieces_ref[piece] = total[:, 128 * piece : 128 * piece + 128]
    hear(round_sem, 2)
    start(to_column)

    convolve(shifted_in, forward_ref, True, mask_ref, out_ref, 3, 4)
    prepare(cotangent_ref, narrow_ref, shifted_grad)
    pad_rows(shifted_grad, padded_grad)
    for copy in halos[8:]:
        copy.wait_recv()
    for copy in halos:
        copy.wait_send()
    place_layers(1, buffers, padded_grad)
    stage_edges(1, buffers, stage_ref)
    place_rows(stage_ref, padded_grad)
    shift_rows(padded_grad, shifted_grad)
    for layer in (0, ROWS + 1):
        shift_layer(padded_grad, shifted_grad, layer, (0, 1, 2))
    convolve(shifted_grad, backward_ref, False, mask_ref, grad_ref, 0, 2)
    arrived(column_bytes, column_sem)
    column_recv[z] = pieces_ref[own]
    piece = column_recv[0]
    for index in range(1, DEEP):
        piece = piece + column_recv[index]
    mine[...] = piece
    start(to_all)

    convolve(shifted_grad, backward_ref, False, mask_ref, grad_ref, 2, 4)
    arrived(gather_bytes, gather_sem)
    back_to_sibling.start()
    left(core_recv, core_sem)
    left(plane_recv, plane_sem)
    left(column_bytes, column_sem)
    left(gather_bytes, gather_sem)
    back_to_sibling.wait()
    cells = lax.axis_size("slab") * lax.axis_size("sub") * ROWS * ROWS * BRICK
    result_ref[...] = full_ref[:, : TAPS * C] * cells ** (-0.5)


def scratch():
    bf16, f32, dma = jnp.bfloat16, jnp.float32, pltpu.SemaphoreType.DMA
    return [
        pltpu.VMEM((ROWS, ROWS, XC), bf16),
        pltpu.VMEM((ROWS, ROWS, XC), bf16),
        pltpu.VMEM((C, TAPS * C), bf16),
        pltpu.SMEM((ROWS // BRICK, ROWS // BRICK), jnp.int32),
        pltpu.VMEM((ROWS // BRICK, ROWS, XC), f32),
        pltpu.VMEM((ROWS // BRICK, ROWS, XC), bf16),
        pltpu.VMEM((ROWS + 2, 48, PADX), f32),
        pltpu.VMEM((ROWS + 2, 48, PADX), f32),
        pltpu.VMEM((2, ROWS, XC), f32),
        pltpu.VMEM((2, ROWS, XC), f32),
        pltpu.VMEM((2, 48, PADX), f32),
        pltpu.VMEM((3, (ROWS + 2) * ROWS, PADX), bf16),
        pltpu.VMEM((3, (ROWS + 2) * ROWS, PADX), bf16),
        pltpu.VMEM((3, 128, 128 * (ROWS + 2)), bf16),
        pltpu.VMEM((2, 128, 128), bf16),
        pltpu.VMEM((256, 9 * WINDOW), bf16),
        pltpu.VMEM((9 * WINDOW, 256), bf16),
        pltpu.VMEM((3, 384, 256), f32),
        pltpu.VMEM((C, WIDE), f32),
        pltpu.VMEM((2, 2, ROWS, XC), bf16),
        pltpu.VMEM((2, 2, ROWS, XC), bf16),
        pltpu.VMEM((2, 2, ROWS, XC), bf16),
        pltpu.VMEM((2, 2, ROWS, XC), bf16),
        pltpu.VMEM((4, 8, XC), f32),
        pltpu.VMEM((4, 8, XC), f32),
        pltpu.VMEM((HALF, WIDE), f32),
        pltpu.VMEM((HALF, WIDE), f32),
        pltpu.VMEM((PLANE - 1, 8, CHUNK), f32),
        pltpu.VMEM((PIECES, 8, 128), f32),
        pltpu.VMEM((DEEP, 8, 128), f32),
        pltpu.VMEM((len(NEAR_STEPS), 8, 128), f32),
        pltpu.VMEM((C, WIDE), f32),
        dma((4,)),
        dma((12,)),
        dma((12,)),
        dma((4,)),
        dma((2,)),
        dma((2,)),
        dma((2,)),
        pltpu.SemaphoreType.REGULAR((3,)),
        pltpu.SemaphoreType.REGULAR((2,)),
    ]


def deliver_kernel(*refs):
    sources, targets, semaphores = refs[:3], refs[3:6], refs[6]
    copies = [
        pltpu.make_async_copy(source, target, semaphores.at[index])
        for index, (source, target) in enumerate(zip(sources, targets))
    ]
    for copy in copies:
        copy.start()
    for copy in copies:
        copy.wait()


def deliver(*arrays):
    return pl.pallas_call(
        deliver_kernel,
        out_shape=[jax.ShapeDtypeStruct(a.shape, a.dtype) for a in arrays],
        in_specs=[pl.BlockSpec(memory_space=pltpu.VMEM)] * 3,
        out_specs=[pl.BlockSpec(memory_space=pltpu.HBM)] * 3,
        scratch_shapes=[pltpu.SemaphoreType.DMA((3,))],
        compiler_params=pltpu.CompilerParams(vmem_limit_bytes=8 * 2**20),
        cost_estimate=pl.CostEstimate(
            flops=0, bytes_accessed=5 * 2**20, transcendentals=0
        ),
        name="deliver",
    )(*arrays)


def per_device(features, cotangent, weight, occupancy):
    hbm = pl.BlockSpec(memory_space=pltpu.HBM)
    out, grad, total = pl.pallas_call(
        kernel,
        out_shape=[
            pltpu.VMEM(features.shape, jnp.bfloat16),
            pltpu.VMEM(features.shape, jnp.bfloat16),
            pltpu.VMEM((C, TAPS * C), jnp.float32),
        ],
        in_specs=[hbm] * 4,
        out_specs=[pl.BlockSpec(memory_space=pltpu.VMEM)] * 3,
        scratch_shapes=scratch(),
        compiler_params=pltpu.CompilerParams(
            collective_id=0, has_side_effects=True, vmem_limit_bytes=55 * 2**20
        ),
        cost_estimate=pl.CostEstimate(
            flops=11 * 10**9, bytes_accessed=5 * 2**20, transcendentals=0
        ),
        name="convolutions",
    )(features, cotangent, weight, occupancy)
    return deliver(out, grad, total)


def solution(mesh):
    placed = (P("slab", "sub", None), P("slab", "sub", None), P(), P("slab", "sub"))
    return jax.shard_map(
        per_device,
        mesh=mesh,
        in_specs=placed,
        out_specs=(P("slab", "sub", None), P("slab", "sub", None), P()),
        check_vma=False,
    )
```
